128 devices in a mesh: row: 8 (over z, x_hi), col: 16 (over x_lo, y, core).
Axes of the slice: x: 4 (x_hi: 2, x_lo: 2; x = x_hi * 2 + x_lo), y: 4, z: 4, core: 2. Of those that a mesh axis runs over, the one named last changes fastest.
Arguments:
- activations: bfloat16 [65536, 4096], P(('row', 'col')), may hold values from -6 to 6
- out_grads: bfloat16 [65536, 14336], P(('row', 'col')), may hold values from -6 to 6
- token_counts: int32 [128, 64], P(('row', 'col')), may hold values from 1 to 16, 512 in all within a row
- proj_seeds: int32 [2], replicated, may hold values from 0 to 29999
Outputs:
- kernel: float32 [8192, 8192], P('row', 'col')
The draws below stay inside these ranges and needn't reach their ends.
Inputs may be any that keep to these rules, and one draw needn't show every extreme that they name: `token_counts`: each row sums to 512.
All inputs are finite; a program needn't handle non-finite values.
Results may differ from the reference program's by a relative error of at most 0.0025.
Values may be sent and summed in bfloat16 or wider, within the bound.
A program may use at most 192 MiB of HBM per device.

```python
import math
import jax
import jax.numpy as jnp
import numpy as np
from jax import lax

D = 4096
FF = 14336
KO = 128
KI = 64
EX_DEV = 64
TOK_DEV = 512
MOST = 16
EXAMPLES = 8192
TOKENS = 65536
N_ROW = 8
N_COL = 16


def levels(rng, shape, cuts, low, largest):
    loudness, own = 1.0, jax.random.fold_in(rng, 6)
    for dim, blocks in cuts:
        heights = jnp.exp(jax.random.uniform(jax.random.fold_in(own, dim), (blocks,), jnp.float32, low / len(cuts), largest / len(cuts)))
        loudness = loudness * jnp.repeat(heights, shape[dim] // blocks).reshape([-1 if axis == dim else 1 for axis in range(len(shape))])
    return loudness


def profile(amount, total, limit, skew):
    loads = [(1 << 20) // math.isqrt(standing ** skew) + 1 for standing in range(2, amount + 1)]
    spare, given = total - limit - (amount - 1), [1] * (amount - 1)
    while spare > 0:
        movable = [i for i in range(amount - 1) if given[i] < limit]
        whole, left = sum([loads[i] for i in movable]), spare
        for i in movable:
            more = min(limit - given[i], max(1, left * loads[i] // whole), spare)
            given[i] = given[i] + more
            spare = spare - more
    return np.array([limit] + given)


def ragged(own_key, amount, total, limit, lean):
    if amount == 2:
        one = jax.random.randint(own_key, (), max(1, total - limit), min(limit, total - 1) + 1)
        return jnp.stack([one, total - one])
    tallies = jnp.asarray(profile(amount, total, limit, lean), jnp.int32)
    twos = (amount - 1) // 2
    giver, sink = tallies[1:1 + 2 * twos:2], tallies[2:2 + 2 * twos:2]
    margin = jnp.minimum(giver - 1, limit - sink)
    moved = jax.random.randint(jax.random.fold_in(own_key, 1), (twos,), 0, 1 << 20) % (margin + 1)
    tallies = tallies.at[1:1 + 2 * twos:2].set(giver - moved).at[2:2 + 2 * twos:2].set(sink + moved)
    return tallies[jax.random.permutation(jax.random.fold_in(own_key, 2), amount)]


def bell_draw(key, dims, spread, most, split=(), kind=jnp.bfloat16):
    array = spread * jax.random.normal(key, dims, jnp.float32)
    if split:
        array = array * levels(key, dims, split, -0.22, 0.18)
    return jnp.clip(array, -most, most).astype(kind)


def setup_inputs(seed: int = 0) -> dict:
    seeds = jax.random.split(jax.random.key(seed), 5)
    activations = bell_draw(seeds[0], (TOKENS, D), 1.0, 6.0, ((0, 128),))
    out_grads = bell_draw(seeds[1], (TOKENS, FF), 1.0, 6.0, ((0, 128),))
    token_counts = jax.vmap(lambda own: ragged(own, EX_DEV, TOK_DEV, MOST, 2))(jax.random.split(seeds[2], (N_ROW * N_COL))).reshape((N_ROW * N_COL, EX_DEV)).astype(jnp.int32)
    proj_seeds = jax.random.randint(seeds[3], (2,), 0, 30000).astype(jnp.int32)
    return {"activations": activations, "out_grads": out_grads, "token_counts": token_counts, "proj_seeds": proj_seeds}


modulus = 32749

def sign_table(table_rows, table_cols, seed_value):
    row_ids = lax.broadcasted_iota(jnp.int32, (table_rows, table_cols), 0)
    col_ids = lax.broadcasted_iota(jnp.int32, (table_rows, table_cols), 1)
    mixed_hash = (row_ids * 181 + col_ids * 7 + seed_value) % modulus
    mixed_hash = (mixed_hash * mixed_hash + 5471) % modulus
    mixed_hash = (mixed_hash * mixed_hash + col_ids * 31 + row_ids) % modulus
    mixed_hash = (mixed_hash * mixed_hash + 12007) % modulus
    return (1 - 2 * (mixed_hash % 2)).astype(jnp.bfloat16)

def device_features(act_block, grad_block, counts, in_signs, out_signs):
    tokens = act_block.shape[0]
    grad_proj = jnp.dot(grad_block.astype(jnp.float32), out_signs.astype(jnp.float32), precision=lax.Precision.HIGHEST, preferred_element_type=jnp.float32) * (1.0 / math.sqrt(FF))
    act_proj = jnp.dot(act_block.astype(jnp.float32), in_signs.astype(jnp.float32), precision=lax.Precision.HIGHEST, preferred_element_type=jnp.float32) * (1.0 / math.sqrt(D))
    outer_terms = (grad_proj[:, :, None] * act_proj[:, None, :]).reshape(tokens, KO * KI)
    end_marks = jnp.cumsum(counts, dtype=jnp.int32)
    starts = end_marks - counts
    places = lax.broadcasted_iota(jnp.int32, (counts.shape[0], tokens), 1)
    member = ((places >= starts[:, None]) & (places < end_marks[:, None])).astype(jnp.float32)
    summed = jnp.dot(member, outer_terms, precision=lax.Precision.HIGHEST, preferred_element_type=jnp.float32)
    return summed.astype(jnp.bfloat16)

def reference(activations, out_grads, token_counts, proj_seeds):
    in_signs = sign_table(D, KI, proj_seeds[0])
    out_signs = sign_table(FF, KO, proj_seeds[1])
    act_blocks = activations.reshape(N_ROW * N_COL, TOK_DEV, D)
    grad_blocks = out_grads.reshape(N_ROW * N_COL, TOK_DEV, FF)

    def one_device(inputs):
        act_block, grad_block, counts = inputs
        return device_features(act_block, grad_block, counts, in_signs, out_signs)
    features = lax.map(one_device, (act_blocks, grad_blocks, token_counts))
    features = lax.optimization_barrier(features.reshape(EXAMPLES, KO * KI))
    widened = features.astype(jnp.float32)
    product = jnp.dot(widened, widened.T, precision=lax.Precision.HIGHEST, preferred_element_type=jnp.float32)
    return product * (1.0 / (KO * KI))
```

```python
import functools
import math

import jax
import jax.numpy as jnp
from jax import lax
from jax.experimental import pallas as pl
from jax.experimental.pallas import tpu as pltpu
from jax.sharding import PartitionSpec as P

KO = 128
KI = 64
MOD = 32749
MESH = pl.DeviceIdType.MESH
F32 = jnp.float32
I32 = jnp.int32
BF16 = jnp.bfloat16
I16 = jnp.int16

TOK = 512
EX = 64
STEPS = 16
ROWS_G = TOK
ROWS_A = ROWS_G + 4 * KI
ROWS = ROWS_A + 4 * 16
LANE = 128


def reduced(x):
    q = (x.astype(F32) * (1.0 / MOD)).astype(I32)
    return x - q * MOD


def signs_of(first, second):
    h = reduced(first * first + 5471)
    h = reduced(h * h + second)
    x = h * h + 12007
    q = (x.astype(F32) * (1.0 / MOD) + 0.5).astype(I32)
    r = x - q * MOD
    odd = (r ^ (r >> 31)) & 1
    return jnp.where(odd == 0, 1.0, -1.0).astype(F32).astype(BF16)


def centred(scalar):
    low = lax.rem(scalar, MOD)
    return jnp.where(low > MOD // 2, low - MOD, low)


def exponent(largest):
    return jnp.ceil(jnp.log2(jnp.maximum(largest, 1e-30)))


def project_kernel(seeds_ref, counts_ref, act_ref, grad_ref, out_ref, g_acc, a_acc, s_g, s_a):
    step = pl.program_id(0)
    depth_g = grad_ref.shape[1]
    depth_a = act_ref.shape[1]

    @pl.when(step == 0)
    def _():
        g_acc[...] = jnp.zeros_like(g_acc)
        a_acc[...] = jnp.zeros_like(a_acc)

    sub = lax.broadcasted_iota(I32, (LANE, KO), 0)
    lane = lax.broadcasted_iota(I32, (LANE, KO), 1)
    for part in range(depth_g // LANE):
        start = step * depth_g + part * LANE
        first = (181 * sub + 7 * lane) + centred(181 * start + seeds_ref[1])
        second = (sub + 31 * lane) + start
        s_g[part * LANE:(part + 1) * LANE, :] = signs_of(first, second)
    sub = lax.broadcasted_iota(I32, (KI, LANE), 0)
    lane = lax.broadcasted_iota(I32, (KI, LANE), 1)
    for part in range(depth_a // LANE):
        start = step * depth_a + part * LANE
        first = (181 * lane + 7 * sub) + centred(181 * start + seeds_ref[0])
        second = (lane + 31 * sub) + start
        s_a[:, part * LANE:(part + 1) * LANE] = signs_of(first, second)
    g_acc[...] += jnp.dot(grad_ref[...], s_g[...], preferred_element_type=F32)
    a_acc[...] += lax.dot_general(
        s_a[...], act_ref[...], (((1,), (1,)), ((), ())), preferred_element_type=F32
    )

    @pl.when(step == STEPS - 1)
    def _():
        g = g_acc[...]
        a = a_acc[...]
        size = jnp.abs(g)
        g_up = exponent(jnp.max(size, axis=1, keepdims=True))
        g_across = exponent(jnp.max(size.T, axis=0, keepdims=True))
        a_up = exponent(jnp.max(jnp.abs(a), axis=0, keepdims=True))
        out_ref[0:ROWS_G, :] = jnp.round(g * jnp.exp2(14.0 - g_up)).astype(I32).astype(I16)
        a = jnp.round(a * jnp.exp2(14.0 - a_up)).astype(I32).astype(I16)
        total = g_across + a_up
        places = lax.broadcasted_iota(I32, (1, TOK), 1)

        def tally(e, carry):
            end, owner = carry
            end = end + counts_ref[0, e]
            return end, owner + (places >= end).astype(I32)

        _, owner = lax.fori_loop(0, EX, tally, (jnp.int32(0), jnp.zeros((1, TOK), I32)))
        row = lax.broadcasted_iota(I32, (16, TOK), 0)
        facts = jnp.where(row == 0, total.astype(I32), jnp.where(row == 1, owner, 0)).astype(I16)
        for k in range(4):
            out_ref[ROWS_G + KI * k:ROWS_G + KI * (k + 1), :] = a[:, LANE * k:LANE * (k + 1)]
            out_ref[ROWS_A + 16 * k:ROWS_A + 16 * (k + 1), :] = facts[:, LANE * k:LANE * (k + 1)]


def project(activations, out_grads, counts, seeds):
    width_a = activations.shape[1] // STEPS
    width_g = out_grads.shape[1] // STEPS
    return pl.pallas_call(
        project_kernel,
        grid=(STEPS,),
        out_shape=jax.ShapeDtypeStruct((ROWS, LANE), I16),
        in_specs=[
            pl.BlockSpec(memory_space=pltpu.SMEM),
            pl.BlockSpec(memory_space=pltpu.SMEM),
            pl.BlockSpec((TOK, width_a), lambda s: (0, s)),
            pl.BlockSpec((TOK, width_g), lambda s: (0, s)),
        ],
        out_specs=pl.BlockSpec((ROWS, LANE), lambda s: (0, 0)),
        scratch_shapes=[
            pltpu.VMEM((TOK, KO), F32),
            pltpu.VMEM((KI, TOK), F32),
            pltpu.VMEM((width_g, KO), BF16),
            pltpu.VMEM((KI, width_a), BF16),
        ],
        compiler_params=pltpu.CompilerParams(vmem_limit_bytes=32 << 20),
        cost_estimate=pl.CostEstimate(flops=4 << 30, bytes_accessed=19 << 20, transcendentals=0),
        name="project",
    )(seeds, counts, activations, out_grads)


def form(held, slot, scale, target, row0, g_hi, g_lo, kin, a_work, hi_ref, lo_ref, lhs):
    g = held[slot, 0:ROWS_G, :].astype(I32).astype(F32)
    high = g.astype(BF16)
    g_hi[...] = high
    g_lo[...] = (g - high.astype(F32)).astype(BF16)
    for k in range(4):
        facts = held[slot, ROWS_A + 16 * k:ROWS_A + 16 * (k + 1), :].astype(I32)
        sizes = jnp.exp2(facts[0:1, :].astype(F32)) * scale
        part = held[slot, ROWS_G + KI * k:ROWS_G + KI * (k + 1), :].astype(I32).astype(F32)
        a_work[k, 0:KI, :] = part * sizes
        a_work[k, KI:KI + 8, :] = jnp.broadcast_to(facts[1:2, :].astype(F32), (8, LANE))
        kin[k] = jnp.broadcast_to((facts[1:2, :] >> 3).astype(F32), (LANE, LANE)).T.astype(BF16)
    sub = lax.broadcasted_iota(I32, (8, LANE), 0)

    def pair(p, carry):
        halves = []
        for half in range(2):
            group = 2 * p + half
            low = (group * 8).astype(F32)
            a = a_work[0]
            for k in range(1, 4):
                owner = a_work[k, KI:KI + 8, :]
                mine = ((owner >= low) & (owner < low + 8.0))[None]
                a = jnp.where(mine, a_work[k].reshape(KI // 8 + 1, 8, LANE), a.reshape(KI // 8 + 1, 8, LANE))
            a = a.reshape(KI + 8, LANE)
            member = a[KI:, :] == low + sub.astype(F32)
            a = a[:KI, :]
            hi = a.astype(BF16).astype(F32)
            hi_ref[half] = hi
            lo_ref[half] = a - hi
            for j in range(0, KI, 2):
                for k, ref in enumerate((hi_ref, lo_ref)):
                    rows = [
                        jnp.where(member, jnp.broadcast_to(ref[half, j + n:j + n + 1, :], (8, LANE)), 0.0)
                        for n in range(2)
                    ]
                    lhs[half, 8 * j:8 * j + 16, LANE * k:LANE * (k + 1)] = jnp.concatenate(rows, 0).astype(BF16)
            this = group.astype(F32).astype(BF16)
            above, below = g_hi[0:LANE, :], g_lo[0:LANE, :]
            for k in range(1, 4):
                mine = kin[k] == this
                above = jnp.where(mine, g_hi[LANE * k:LANE * (k + 1), :], above)
                below = jnp.where(mine, g_lo[LANE * k:LANE * (k + 1), :], below)
            weights = jnp.concatenate([above, below], axis=1)
            weights = jnp.concatenate([weights, weights], axis=0)
            both = jnp.dot(lhs[half], weights, preferred_element_type=F32)
            halves.append((both[:, :LANE] + both[:, LANE:]).reshape(KI, 8, LANE))
        features = jnp.concatenate(halves, axis=1).astype(BF16)
        at = pl.multiple_of(row0 + p * 16, 16)
        for j in range(KI):
            target[pl.ds(at, 16), LANE * j:LANE * (j + 1)] = features[j]
        return carry

    lax.fori_loop(0, 4, pair, 0)


def panel_kernel(n_row, n_col, packed_ref, out_ref, held, left, right,
                 g_hi, g_lo, kin, a_work, hi_ref, lo_ref, lhs, own_sem, send_row, send_col, arrive):
    r = lax.axis_index("row")
    c = lax.axis_index("col")
    span = n_col // n_row
    per = n_col // span
    panel = r * span + c // per
    home = c // span
    first = lax.rem(c, span) * per
    crossing = home != r

    barrier = pltpu.get_barrier_semaphore()
    for k in range(1, n_col):
        pl.semaphore_signal(barrier, inc=1, device_id=(r, lax.rem(c + k, n_col)), device_id_type=MESH)
    for k in range(1, n_row):
        pl.semaphore_signal(barrier, inc=1, device_id=(lax.rem(r + k, n_row), panel), device_id_type=MESH)

    @pl.when(crossing)
    def _():
        for k in range(per):
            pl.semaphore_signal(barrier, inc=1, device_id=(home, first + k), device_id_type=MESH)

    pl.semaphore_wait(barrier, n_col - 1 + n_row - 1 + jnp.where(crossing, per, 0))

    own = pltpu.make_async_copy(packed_ref, held.at[c], own_sem)
    own.start()

    def to_row(k):
        other = lax.rem(c + k, n_col)
        return pltpu.make_async_remote_copy(
            src_ref=packed_ref, dst_ref=held.at[c], send_sem=send_row.at[k - 1], recv_sem=arrive.at[c],
            device_id=(r, other), device_id_type=MESH)

    def to_col(k):
        slot = n_col + lax.rem(c, per)
        return pltpu.make_async_remote_copy(
            src_ref=packed_ref, dst_ref=held.at[slot], send_sem=send_col.at[k - 1], recv_sem=arrive.at[slot],
            device_id=(lax.rem(r + k, n_row), panel), device_id_type=MESH)

    for k in range(1, n_row):
        to_col(k).start()
    for k in range(1, n_col):
        to_row(k).start()

    work = (g_hi, g_lo, kin, a_work, hi_ref, lo_ref, lhs)
    unit = 2.0 ** -28 / 64.0
    scale = unit / math.sqrt(14336.0)

    def landed(slot):
        pltpu.make_async_remote_copy(
            src_ref=held.at[slot], dst_ref=held.at[slot], send_sem=own_sem, recv_sem=arrive.at[slot],
            device_id=(r, c), device_id_type=MESH).wait_recv()

    own.wait()
    form(held, c, scale / 64.0, left, c * EX, *work)

    def row_block(k, carry):
        slot = lax.rem(c + k, n_col)
        landed(slot)
        form(held, slot, scale / 64.0, left, slot * EX, *work)
        return carry

    lax.fori_loop(1, n_col, row_block, 0)

    def col_block(k, carry):
        @pl.when(crossing)
        def _():
            landed(n_col + k)

        slot = jnp.where(crossing, n_col + k, first + k)
        form(held, slot, scale / 128.0, right, k * EX, *work)
        return carry

    lax.fori_loop(0, per, col_block, 0)

    def tile(t, carry):
        at = pl.multiple_of(t * 256, 256)
        total = None
        for k in range(4):
            term = lax.dot_general(
                left[pl.ds(at, 256), 2048 * k:2048 * (k + 1)], right[:, 2048 * k:2048 * (k + 1)],
                (((1,), (1,)), ((), ())), preferred_element_type=F32)
            total = term if total is None else total + term
        out_ref[pl.ds(at, 256), :] = total
        return carry

    lax.fori_loop(0, 4, tile, 0)

    for k in range(1, n_row):
        to_col(k).wait_send()
    for k in range(1, n_col):
        to_row(k).wait_send()


def panels(packed, n_row, n_col):
    per = n_row
    rows, cols = n_col * EX, per * EX
    return pl.pallas_call(
        functools.partial(panel_kernel, n_row, n_col),
        out_shape=jax.ShapeDtypeStruct((rows, cols), F32),
        in_specs=[pl.BlockSpec(memory_space=pltpu.VMEM)],
        out_specs=pl.BlockSpec(memory_space=pltpu.VMEM),
        scratch_shapes=[
            pltpu.VMEM((n_col + per, ROWS, LANE), I16),
            pltpu.VMEM((rows, KO * KI), BF16),
            pltpu.VMEM((cols, KO * KI), BF16),
            pltpu.VMEM((TOK, KO), BF16),
            pltpu.VMEM((TOK, KO), BF16),
            pltpu.VMEM((4, LANE, LANE), BF16),
            pltpu.VMEM((4, KI + 8, LANE), F32),
            pltpu.VMEM((2, KI, LANE), F32),
            pltpu.VMEM((2, KI, LANE), F32),
            pltpu.VMEM((2, 8 * KI, 2 * LANE), BF16),
            pltpu.SemaphoreType.DMA,
            pltpu.SemaphoreType.DMA((n_col - 1,)),
            pltpu.SemaphoreType.DMA((n_row - 1,)),
            pltpu.SemaphoreType.DMA((n_col + per,)),
        ],
        compiler_params=pltpu.CompilerParams(
            collective_id=0, has_side_effects=True, vmem_limit_bytes=56 << 20),
        cost_estimate=pl.CostEstimate(flops=20 << 30, bytes_accessed=4 << 20, transcendentals=0),
        name="panels",
    )(packed)


def body(n_row, n_col, activations, out_grads, token_counts, proj_seeds):
    packed = project(activations, out_grads, token_counts, proj_seeds)
    return panels(packed, n_row, n_col)


def solution(mesh):
    return jax.shard_map(
        functools.partial(body, mesh.shape["row"], mesh.shape["col"]),
        mesh=mesh,
        in_specs=(P(("row", "col"), None), P(("row", "col"), None), P(("row", "col"), None), P()),
        out_specs=P("row", "col"),
        check_vma=False,
    )
```

```python
import functools
import math

import jax
import jax.numpy as jnp
from jax import lax
from jax.experimental import pallas as pl
from jax.experimental.pallas import tpu as pltpu
from jax.sharding import PartitionSpec as P

KO = 128
KI = 64
MOD = 32749
MESH = pl.DeviceIdType.MESH
F32 = jnp.float32
I32 = jnp.int32
BF16 = jnp.bfloat16
I16 = jnp.int16

TOK = 512
EX = 64
STEPS = 16
ROWS_G = TOK
ROWS_A = ROWS_G + 4 * KI
ROWS = ROWS_A + 4 * 16
LANE = 128


def reduced(x):
    q = (x.astype(F32) * (1.0 / MOD)).astype(I32)
    return x - q * MOD


def signs_of(first, second):
    h = reduced(first * first + 5471)
    h = reduced(h * h + second)
    x = h * h + 12007
    q = (x.astype(F32) * (1.0 / MOD) + 0.5).astype(I32)
    r = x - q * MOD
    odd = (r ^ (r >> 31)) & 1
    return jnp.where(odd == 0, 1.0, -1.0).astype(F32).astype(BF16)


def centred(scalar):
    low = lax.rem(scalar, MOD)
    return jnp.where(low > MOD // 2, low - MOD, low)


def exponent(largest):
    return jnp.ceil(jnp.log2(jnp.maximum(largest, 1e-30)))


def project_kernel(seeds_ref, counts_ref, act_ref, grad_ref, out_ref, g_acc, a_acc, s_g, s_a):
    step = pl.program_id(0)
    depth_g = grad_ref.shape[1]
    depth_a = act_ref.shape[1]

    @pl.when(step == 0)
    def _():
        g_acc[...] = jnp.zeros_like(g_acc)
        a_acc[...] = jnp.zeros_like(a_acc)

    sub = lax.broadcasted_iota(I32, (LANE, KO), 0)
    lane = lax.broadcasted_iota(I32, (LANE, KO), 1)
    for part in range(depth_g // LANE):
        start = step * depth_g + part * LANE
        first = (181 * sub + 7 * lane) + centred(181 * start + seeds_ref[1])
        second = (sub + 31 * lane) + start
        s_g[part * LANE:(part + 1) * LANE, :] = signs_of(first, second)
    sub = lax.broadcasted_iota(I32, (KI, LANE), 0)
    lane = lax.broadcasted_iota(I32, (KI, LANE), 1)
    for part in range(depth_a // LANE):
        start = step * depth_a + part * LANE
        first = (181 * lane + 7 * sub) + centred(181 * start + seeds_ref[0])
        second = (lane + 31 * sub) + start
        s_a[:, part * LANE:(part + 1) * LANE] = signs_of(first, second)
    g_acc[...] += jnp.dot(grad_ref[...], s_g[...], preferred_element_type=F32)
    a_acc[...] += lax.dot_general(
        s_a[...], act_ref[...], (((1,), (1,)), ((), ())), preferred_element_type=F32
    )

    @pl.when(step == STEPS - 1)
    def _():
        g = g_acc[...]
        a = a_acc[...]
        size = jnp.abs(g)
        g_up = exponent(jnp.max(size, axis=1, keepdims=True))
        g_across = exponent(jnp.max(size.T, axis=0, keepdims=True))
        a_up = exponent(jnp.max(jnp.abs(a), axis=0, keepdims=True))
        out_ref[0:ROWS_G, :] = jnp.round(g * jnp.exp2(14.0 - g_up)).astype(I32).astype(I16)
        a = jnp.round(a * jnp.exp2(14.0 - a_up)).astype(I32).astype(I16)
        total = g_across + a_up
        places = lax.broadcasted_iota(I32, (1, TOK), 1)

        def tally(e, carry):
            end, owner = carry
            end = end + counts_ref[0, e]
            return end, owner + (places >= end).astype(I32)

        _, owner = lax.fori_loop(0, EX, tally, (jnp.int32(0), jnp.zeros((1, TOK), I32)))
        row = lax.broadcasted_iota(I32, (16, TOK), 0)
        facts = jnp.where(row == 0, total.astype(I32), jnp.where(row == 1, owner, 0)).astype(I16)
        for k in range(4):
            out_ref[ROWS_G + KI * k:ROWS_G + KI * (k + 1), :] = a[:, LANE * k:LANE * (k + 1)]
            out_ref[ROWS_A + 16 * k:ROWS_A + 16 * (k + 1), :] = facts[:, LANE * k:LANE * (k + 1)]


def project(activations, out_grads, counts, seeds):
    width_a = activations.shape[1] // STEPS
    width_g = out_grads.shape[1] // STEPS
    return pl.pallas_call(
        project_kernel,
        grid=(STEPS,),
        out_shape=jax.ShapeDtypeStruct((ROWS, LANE), I16),
        in_specs=[
            pl.BlockSpec(memory_space=pltpu.SMEM),
            pl.BlockSpec(memory_space=pltpu.SMEM),
            pl.BlockSpec((TOK, width_a), lambda s: (0, s)),
            pl.BlockSpec((TOK, width_g), lambda s: (0, s)),
        ],
        out_specs=pl.BlockSpec((ROWS, LANE), lambda s: (0, 0)),
        scratch_shapes=[
            pltpu.VMEM((TOK, KO), F32),
            pltpu.VMEM((KI, TOK), F32),
            pltpu.VMEM((width_g, KO), BF16),
            pltpu.VMEM((KI, width_a), BF16),
        ],
        compiler_params=pltpu.CompilerParams(vmem_limit_bytes=60 << 20),
        cost_estimate=pl.CostEstimate(flops=4 << 30, bytes_accessed=19 << 20, transcendentals=0),
        name="project",
    )(seeds, counts, activations, out_grads)


def form(held, slot, scale, target, row0, g_hi, g_lo, kin, a_work, hi_ref, lo_ref, lhs):
    g = held[slot, 0:ROWS_G, :].astype(I32).astype(F32)
    high = g.astype(BF16)
    g_hi[...] = high
    g_lo[...] = (g - high.astype(F32)).astype(BF16)
    for k in range(4):
        facts = held[slot, ROWS_A + 16 * k:ROWS_A + 16 * (k + 1), :].astype(I32)
        sizes = jnp.exp2(facts[0:1, :].astype(F32)) * scale
        part = held[slot, ROWS_G + KI * k:ROWS_G + KI * (k + 1), :].astype(I32).astype(F32)
        a_work[k, 0:KI, :] = part * sizes
        a_work[k, KI:KI + 8, :] = jnp.broadcast_to(facts[1:2, :].astype(F32), (8, LANE))
        kin[k] = jnp.broadcast_to((facts[1:2, :] >> 3).astype(F32), (LANE, LANE)).T.astype(BF16)
    sub = lax.broadcasted_iota(I32, (8, LANE), 0)

    def pair(p, carry):
        halves = []
        for half in range(2):
            group = 2 * p + half
            low = (group * 8).astype(F32)
            a = a_work[0]
            for k in range(1, 4):
                owner = a_work[k, KI:KI + 8, :]
                mine = ((owner >= low) & (owner < low + 8.0))[None]
                a = jnp.where(mine, a_work[k].reshape(KI // 8 + 1, 8, LANE), a.reshape(KI // 8 + 1, 8, LANE))
            a = a.reshape(KI + 8, LANE)
            member = a[KI:, :] == low + sub.astype(F32)
            a = a[:KI, :]
            hi = a.astype(BF16).astype(F32)
            hi_ref[half] = hi
            lo_ref[half] = a - hi
            for j in range(0, KI, 2):
                for k, ref in enumerate((hi_ref, lo_ref)):
                    rows = [
                        jnp.where(member, jnp.broadcast_to(ref[half, j + n:j + n + 1, :], (8, LANE)), 0.0)
                        for n in range(2)
                    ]
                    lhs[half, 8 * j:8 * j + 16, LANE * k:LANE * (k + 1)] = jnp.concatenate(rows, 0).astype(BF16)
            this = group.astype(F32).astype(BF16)
            above, below = g_hi[0:LANE, :], g_lo[0:LANE, :]
            for k in range(1, 4):
                mine = kin[k] == this
                above = jnp.where(mine, g_hi[LANE * k:LANE * (k + 1), :], above)
                below = jnp.where(mine, g_lo[LANE * k:LANE * (k + 1), :], below)
            weights = jnp.concatenate([above, below], axis=1)
            weights = jnp.concatenate([weights, weights], axis=0)
            both = jnp.dot(lhs[half], weights, preferred_element_type=F32)
            halves.append((both[:, :LANE] + both[:, LANE:]).reshape(KI, 8, LANE))
        features = jnp.concatenate(halves, axis=1).astype(BF16)
        at = pl.multiple_of(row0 + p * 16, 16)
        for j in range(KI):
            target[pl.ds(at, 16), LANE * j:LANE * (j + 1)] = features[j]
        return carry

    lax.fori_loop(0, 4, pair, 0)


def panel_kernel(n_row, n_col, packed_ref, out_ref, held, panel, g_hi, g_lo, kin, a_work, hi_ref, lo_ref, lhs,
                 send, arrive):
    p = lax.axis_index("row")
    core = lax.rem(lax.axis_index("col"), 2)
    q = lax.axis_index("col") // 2
    chips = n_col // 2
    diagonal = p == q

    def pair_q(m):
        return lax.rem(m + 4, 8)

    def ring_q(m, k):
        return (m // 4) * 4 + lax.rem(m + k, 4)

    def pair_p(m):
        return m + 1 - 2 * lax.rem(m, 2)

    def ring_p(m, k):
        return lax.rem(m + 2 * k, 8)

    sibling = (p, 2 * q + 1 - core)
    flipped = (q, 2 * p + core)
    row_pair, row_up, row_down = [(p, 2 * m + core) for m in (pair_q(q), ring_q(q, 1), ring_q(q, 3))]
    col_pair, col_up, col_down = [(m, 2 * q + core) for m in (pair_p(p), ring_p(p, 1), ring_p(p, 3))]

    barrier = pltpu.get_barrier_semaphore()
    for other in (sibling, row_pair, row_up, row_down, col_pair, col_up, col_down):
        pl.semaphore_signal(barrier, inc=1, device_id=other, device_id_type=MESH)

    @pl.when(jnp.logical_not(diagonal))
    def _():
        pl.semaphore_signal(barrier, inc=1, device_id=flipped, device_id_type=MESH)

    pl.semaphore_wait(barrier, jnp.where(diagonal, 7, 8))

    def row_slot(m):
        return 2 * m + core

    def col_slot(m):
        return n_col + 2 * m + core

    def copy(number, source, slot, device):
        return pltpu.make_async_remote_copy(
            src_ref=source, dst_ref=held.at[slot], send_sem=send.at[number], recv_sem=arrive.at[slot],
            device_id=device, device_id_type=MESH)

    def landed(slot):
        copy(0, held.at[slot], slot, sibling).wait_recv()

    own_slot = row_slot(q)
    rows = [q, pair_q(q), ring_q(q, 3), ring_q(q, 1), pair_q(ring_q(q, 3)), pair_q(ring_q(q, 1)), ring_q(q, 2),
            pair_q(ring_q(q, 2))]
    cols = [p, pair_p(p), ring_p(p, 3), ring_p(p, 1), pair_p(ring_p(p, 3)), pair_p(ring_p(p, 1)), ring_p(p, 2),
            pair_p(ring_p(p, 2))]
    row_next = {0: (row_pair, row_up, row_down), 1: (row_up, row_down), 2: (row_up,), 5: (row_down,)}
    col_next = {0: (col_pair, col_up, col_down), 1: (col_up, col_down), 2: (col_up,), 5: (col_down,)}

    def row_sends(i):
        slot = row_slot(rows[i])
        source = packed_ref if i == 0 else held.at[slot]
        base = 0 if i == 0 else sum(len(row_next.get(n, ())) + 1 for n in range(i))
        return [copy(base + n, source, slot, device) for n, device in enumerate(row_next.get(i, ()) + (sibling,))]

    def col_sends(i):
        slot = col_slot(cols[i])
        base = 16 + sum(len(col_next.get(n, ())) + 1 for n in range(i))
        moves = [copy(base + n, held.at[slot], slot, device) for n, device in enumerate(col_next.get(i, ()))]
        return moves, copy(base + len(moves), held.at[slot], slot, sibling), cols[i] // 4 != core

    flip = pltpu.make_async_remote_copy(
        src_ref=packed_ref, dst_ref=held.at[col_slot(q)], send_sem=send.at[15], recv_sem=arrive.at[col_slot(q)],
        device_id=flipped, device_id_type=MESH)
    stay = pltpu.make_async_copy(packed_ref, held.at[col_slot(q)], arrive.at[col_slot(q)])

    @pl.when(jnp.logical_not(diagonal))
    def _():
        flip.start()

    @pl.when(diagonal)
    def _():
        stay.start()

    for move in row_sends(0):
        move.start()
    own = pltpu.make_async_copy(packed_ref, held.at[own_slot], arrive.at[own_slot])
    own.start()

    def row_step(i):
        landed(row_slot(rows[i]))
        if i > 0:
            for move in row_sends(i):
                move.start()

    def col_step(i):
        landed(col_slot(cols[i]))
        moves, across, wanted = col_sends(i)
        for move in moves:
            move.start()

        @pl.when(wanted)
        def _():
            across.start()

    plan = {0: [(row_step, 0)], 2: [(row_step, 1), (col_step, 0)], 4: [(row_step, 2), (row_step, 3)],
            6: [(col_step, 1), (row_step, 4), (row_step, 5)], 8: [(col_step, 2), (col_step, 3)],
            10: [(row_step, 6)], 11: [(col_step, 5), (col_step, 4)], 12: [(row_step, 7)], 14: [(col_step, 6)],
            16: [(col_step, 7)]}
    unit = 2.0 ** -28 / 64.0
    scale = unit / math.sqrt(14336.0)

    def pick(values, i):
        value = values[0]
        for n in range(1, len(values)):
            value = jnp.where(i == n, values[n], value)
        return value

    def block(k, carry):
        for at, steps in plan.items():
            @pl.when(k == at)
            def _():
                for step, i in steps:
                    step(i)

        is_row = k < n_col
        place = jnp.where(is_row, k, k - n_col) // 2
        other = lax.rem(k, 2)
        part = jnp.where(other == 0, core, 1 - core)
        m = jnp.where(is_row, pick(rows, place), 4 * core + place)
        slot = jnp.where(is_row, 0, n_col) + 2 * m + part

        @pl.when(other == 1)
        def _():
            landed(slot)

        row0 = jnp.where(is_row, slot, n_col + lax.rem(slot, 8)) * EX
        form(held, slot, jnp.where(is_row, scale / 64.0, scale / 128.0), panel, row0,
             g_hi, g_lo, kin, a_work, hi_ref, lo_ref, lhs)
        return carry

    lax.fori_loop(0, n_col + 8, block, 0)

    def tile(t, carry):
        at = pl.multiple_of(t * 256, 256)
        total = None
        for k in range(4):
            term = lax.dot_general(
                panel[pl.ds(at, 256), 2048 * k:2048 * (k + 1)], panel[n_col * EX:, 2048 * k:2048 * (k + 1)],
                (((1,), (1,)), ((), ())), preferred_element_type=F32)
            total = term if total is None else total + term
        out_ref[pl.ds(at, 256), :] = total
        return carry

    lax.fori_loop(0, 4, tile, 0)

    @pl.when(jnp.logical_not(diagonal))
    def _():
        flip.wait_send()

    for i in range(chips):
        for move in row_sends(i):
            move.wait_send()
        moves, across, wanted = col_sends(i)
        for move in moves:
            move.wait_send()

        @pl.when(wanted)
        def _():
            across.wait_send()


def panels(packed, n_row, n_col):
    per = n_row
    rows, cols = n_col * EX, per * EX
    return pl.pallas_call(
        functools.partial(panel_kernel, n_row, n_col),
        out_shape=jax.ShapeDtypeStruct((rows, cols), F32),
        in_specs=[pl.BlockSpec(memory_space=pltpu.VMEM)],
        out_specs=pl.BlockSpec(memory_space=pltpu.VMEM),
        scratch_shapes=[
            pltpu.VMEM((2 * n_col, ROWS, LANE), I16),
            pltpu.VMEM((rows + cols, KO * KI), BF16),
            pltpu.VMEM((TOK, KO), BF16),
            pltpu.VMEM((TOK, KO), BF16),
            pltpu.VMEM((4, LANE, LANE), BF16),
            pltpu.VMEM((4, KI + 8, LANE), F32),
            pltpu.VMEM((2, KI, LANE), F32),
            pltpu.VMEM((2, KI, LANE), F32),
            pltpu.VMEM((2, 8 * KI, 2 * LANE), BF16),
            pltpu.SemaphoreType.DMA((32,)),
            pltpu.SemaphoreType.DMA((2 * n_col,)),
        ],
        compiler_params=pltpu.CompilerParams(
            collective_id=0, has_side_effects=True, vmem_limit_bytes=56 << 20),
        cost_estimate=pl.CostEstimate(flops=20 << 30, bytes_accessed=4 << 20, transcendentals=0),
        name="panels",
    )(packed)


def body(n_row, n_col, activations, out_grads, token_counts, proj_seeds):
    packed = project(activations, out_grads, token_counts, proj_seeds)
    return panels(packed, n_row, n_col)


def solution(mesh):
    return jax.shard_map(
        functools.partial(body, mesh.shape["row"], mesh.shape["col"]),
        mesh=mesh,
        in_specs=(P(("row", "col"), None), P(("row", "col"), None), P(("row", "col"), None), P()),
        out_specs=P("row", "col"),
        check_vma=False,
    )
```

```python
import functools
import math

import jax
import jax.numpy as jnp
from jax import lax
from jax.experimental import pallas as pl
from jax.experimental.pallas import tpu as pltpu
from jax.sharding import PartitionSpec as P

KO = 128
KI = 64
MOD = 32749
MESH = pl.DeviceIdType.MESH
F32 = jnp.float32
I32 = jnp.int32
BF16 = jnp.bfloat16
I16 = jnp.int16

TOK = 512
EX = 64
STEPS = 7
AHEAD = 2
ROWS_G = TOK
ROWS_A = ROWS_G + 4 * KI
ROWS = ROWS_A + 4 * 16
LANE = 128


def reduced(x):
    q = (x.astype(F32) * (1.0 / MOD)).astype(I32)
    return x - q * MOD


def signs_of(first, second):
    h = reduced(first * first + 5471)
    h = reduced(h * h + second)
    x = h * h + 12007
    q = (x.astype(F32) * (1.0 / MOD) + 0.5).astype(I32)
    r = x - q * MOD
    odd = (r ^ (r >> 31)) & 1
    return jnp.where(odd == 0, 1.0, -1.0).astype(F32).astype(BF16)


def centred(scalar):
    low = lax.rem(scalar, MOD)
    return jnp.where(low > MOD // 2, low - MOD, low)


def exponent(largest):
    return jnp.ceil(jnp.log2(jnp.maximum(largest, 1e-30)))


def project_kernel(seeds_ref, counts_ref, act_hbm, grad_hbm, out_ref, act, grad, g_acc, a_acc, s_a, act_sem, grad_sem):
    depth_g = grad.shape[1] // STEPS
    depth_a = act.shape[1] // 8

    def fetch_a(k):
        span = pl.ds(k * (act.shape[1] // 4), act.shape[1] // 4)
        return pltpu.make_async_copy(act_hbm.at[:, span], act.at[:, span], act_sem.at[k])

    def fetch_g(k):
        span = pl.ds(pl.multiple_of(k * depth_g, LANE), depth_g)
        return pltpu.make_async_copy(grad_hbm.at[:, span], grad.at[:, span], grad_sem.at[k])

    for k in range(AHEAD):
        fetch_g(k).start()
    g_acc[...] = jnp.zeros_like(g_acc)
    sub_a = lax.broadcasted_iota(I32, (KI, LANE), 0)
    lane_a = lax.broadcasted_iota(I32, (KI, LANE), 1)

    def part_a(k, carry):
        for part in range(depth_a // LANE):
            start = k * depth_a + part * LANE
            first = (181 * lane_a + 7 * sub_a) + centred(181 * start + seeds_ref[0])
            second = (lane_a + 31 * sub_a) + start
            s_a[:, pl.ds(pl.multiple_of(start, LANE), LANE)] = signs_of(first, second)
        return carry

    lax.fori_loop(0, 8, part_a, 0)
    sub = lax.broadcasted_iota(I32, (LANE, KO), 0)
    lane = lax.broadcasted_iota(I32, (LANE, KO), 1)

    def part_g(k, carry):
        fetch_g(k).wait()

        @pl.when(k + AHEAD < STEPS)
        def _():
            fetch_g(k + AHEAD).start()

        for n in range(4):
            @pl.when(k == n + 1)
            def _():
                fetch_a(n).start()

        signs = []
        for part in range(depth_g // LANE):
            start = k * depth_g + part * LANE
            first = (181 * sub + 7 * lane) + centred(181 * start + seeds_ref[1])
            second = (sub + 31 * lane) + start
            signs.append(signs_of(first, second))
        span = pl.ds(pl.multiple_of(k * depth_g, LANE), depth_g)
        g_acc[...] += jnp.dot(grad[:, span], jnp.concatenate(signs, axis=0), preferred_element_type=F32)
        return carry

    lax.fori_loop(0, STEPS, part_g, 0)
    for k in range(4):
        fetch_a(k).wait()
    a_acc[...] = lax.dot_general(
        s_a[...], act[...], (((1,), (1,)), ((), ())), preferred_element_type=F32
    )
    g = g_acc[...]
    a = a_acc[...]
    size = jnp.abs(g)
    g_up = exponent(jnp.max(size, axis=1, keepdims=True))
    g_across = exponent(jnp.max(size.T, axis=0, keepdims=True))
    a_up = exponent(jnp.max(jnp.abs(a), axis=0, keepdims=True))
    out_ref[0:ROWS_G, :] = jnp.round(g * jnp.exp2(14.0 - g_up)).astype(I32).astype(I16)
    a = jnp.round(a * jnp.exp2(14.0 - a_up)).astype(I32).astype(I16)
    total = g_across + a_up
    places = lax.broadcasted_iota(I32, (1, TOK), 1)

    def tally(e, carry):
        end, owner = carry
        end = end + counts_ref[0, e]
        return end, owner + (places >= end).astype(I32)

    _, owner = lax.fori_loop(0, EX, tally, (jnp.int32(0), jnp.zeros((1, TOK), I32)))
    row = lax.broadcasted_iota(I32, (16, TOK), 0)
    facts = jnp.where(row == 0, total.astype(I32), jnp.where(row == 1, owner, 0)).astype(I16)
    for k in range(4):
        out_ref[ROWS_G + KI * k:ROWS_G + KI * (k + 1), :] = a[:, LANE * k:LANE * (k + 1)]
        out_ref[ROWS_A + 16 * k:ROWS_A + 16 * (k + 1), :] = facts[:, LANE * k:LANE * (k + 1)]


def project(activations, out_grads, counts, seeds):
    depth_a = activations.shape[1]
    depth_g = out_grads.shape[1]
    return pl.pallas_call(
        project_kernel,
        out_shape=jax.ShapeDtypeStruct((ROWS, LANE), I16),
        in_specs=[
            pl.BlockSpec(memory_space=pltpu.SMEM),
            pl.BlockSpec(memory_space=pltpu.SMEM),
            pl.BlockSpec(memory_space=pl.ANY),
            pl.BlockSpec(memory_space=pl.ANY),
        ],
        out_specs=pl.BlockSpec(memory_space=pltpu.VMEM),
        scratch_shapes=[
            pltpu.VMEM((TOK, depth_a), BF16),
            pltpu.VMEM((TOK, depth_g), BF16),
            pltpu.VMEM((TOK, KO), F32),
            pltpu.VMEM((KI, TOK), F32),
            pltpu.VMEM((KI, depth_a), BF16),
            pltpu.SemaphoreType.DMA((4,)),
            pltpu.SemaphoreType.DMA((STEPS,)),
        ],
        compiler_params=pltpu.CompilerParams(vmem_limit_bytes=60 << 20),
        cost_estimate=pl.CostEstimate(flops=4 << 30, bytes_accessed=19 << 20, transcendentals=0),
        name="project",
    )(seeds, counts, activations, out_grads)


def form(held, slot, scale, target, row0, g_hi, g_lo, kin, a_work, hi_ref, lo_ref, lhs):
    g = held[slot, 0:ROWS_G, :].astype(I32).astype(F32)
    high = g.astype(BF16)
    g_hi[...] = high
    g_lo[...] = (g - high.astype(F32)).astype(BF16)
    for k in range(4):
        facts = held[slot, ROWS_A + 16 * k:ROWS_A + 16 * (k + 1), :].astype(I32)
        sizes = jnp.exp2(facts[0:1, :].astype(F32)) * scale
        part = held[slot, ROWS_G + KI * k:ROWS_G + KI * (k + 1), :].astype(I32).astype(F32)
        a_work[k, 0:KI, :] = part * sizes
        a_work[k, KI:KI + 8, :] = jnp.broadcast_to(facts[1:2, :].astype(F32), (8, LANE))
        kin[k] = jnp.broadcast_to((facts[1:2, :] >> 3).astype(F32), (LANE, LANE)).T.astype(BF16)
    sub = lax.broadcasted_iota(I32, (16, LANE), 0) & 7
    halves = []
    for group in range(8):
        low = 8 * group
        near = max(low, LANE * (group - 4)) // LANE
        far = (min(LANE * (group + 1), TOK - 8 * (7 - group)) - 1) // LANE
        a = a_work[near].reshape(KI // 8 + 1, 8, LANE)
        above, below = g_hi[LANE * near:LANE * (near + 1), :], g_lo[LANE * near:LANE * (near + 1), :]
        for k in range(near + 1, far + 1):
            owner = a_work[k, KI:KI + 8, :]
            mine = ((owner >= float(low)) & (owner < float(low + 8)))[None]
            a = jnp.where(mine, a_work[k].reshape(KI // 8 + 1, 8, LANE), a)
            mine = kin[k] == jnp.bfloat16(group)
            above = jnp.where(mine, g_hi[LANE * k:LANE * (k + 1), :], above)
            below = jnp.where(mine, g_lo[LANE * k:LANE * (k + 1), :], below)
        owner = jnp.concatenate([a[KI // 8]] * 2, axis=0)
        member = jnp.where(owner == (sub + low).astype(F32), 1.0, 0.0).astype(BF16)
        a = a[:KI // 8].reshape(KI, LANE)
        hi = a.astype(BF16).astype(F32)
        hi_ref[group] = hi
        lo_ref[group] = a - hi
        for j in range(0, KI, 2):
            for k, ref in enumerate((hi_ref, lo_ref)):
                rows = [jnp.broadcast_to(ref[group, j + n:j + n + 1, :], (8, LANE)) for n in range(2)]
                tile = jnp.concatenate(rows, axis=0).astype(BF16) * member
                lhs[group, 8 * j:8 * j + 16, LANE * k:LANE * (k + 1)] = tile
        weights = jnp.concatenate([above, below], axis=1)
        weights = jnp.concatenate([weights, weights], axis=0)
        both = jnp.dot(lhs[group], weights, preferred_element_type=F32)
        halves.append((both[:, :LANE] + both[:, LANE:]).reshape(KI, 8, LANE))
        if group % 2 == 1:
            features = jnp.concatenate(halves, axis=1).astype(BF16)
            halves = []
            at = pl.multiple_of(row0 + (group // 2) * 16, 16)
            for j in range(KI):
                target[pl.ds(at, 16), LANE * j:LANE * (j + 1)] = features[j]


def panel_kernel(n_row, n_col, packed_ref, out_ref, held, panel, g_hi, g_lo, kin, a_work, hi_ref, lo_ref, lhs,
                 send, arrive):
    p = lax.axis_index("row")
    core = lax.rem(lax.axis_index("col"), 2)
    q = lax.axis_index("col") // 2
    chips = n_col // 2
    diagonal = p == q

    def pair_q(m):
        return lax.rem(m + 4, 8)

    def ring_q(m, k):
        return (m // 4) * 4 + lax.rem(m + k, 4)

    def pair_p(m):
        return m + 1 - 2 * lax.rem(m, 2)

    def ring_p(m, k):
        return lax.rem(m + 2 * k, 8)

    sibling = (p, 2 * q + 1 - core)
    flipped = (q, 2 * p + core)
    row_pair, row_up, row_down = [(p, 2 * m + core) for m in (pair_q(q), ring_q(q, 1), ring_q(q, 3))]
    col_pair, col_up, col_down = [(m, 2 * q + core) for m in (pair_p(p), ring_p(p, 1), ring_p(p, 3))]

    barrier = pltpu.get_barrier_semaphore()
    for other in (sibling, row_pair, row_up, row_down, col_pair, col_up, col_down):
        pl.semaphore_signal(barrier, inc=1, device_id=other, device_id_type=MESH)

    @pl.when(jnp.logical_not(diagonal))
    def _():
        pl.semaphore_signal(barrier, inc=1, device_id=flipped, device_id_type=MESH)

    pl.semaphore_wait(barrier, jnp.where(diagonal, 7, 8))

    def row_slot(m):
        return 2 * m + core

    def col_slot(m):
        return n_col + 2 * m + core

    def copy(number, source, slot, device):
        return pltpu.make_async_remote_copy(
            src_ref=source, dst_ref=held.at[slot], send_sem=send.at[number], recv_sem=arrive.at[slot],
            device_id=device, device_id_type=MESH)

    def landed(slot):
        copy(0, held.at[slot], slot, sibling).wait_recv()

    own_slot = row_slot(q)
    rows = [q, pair_q(q), ring_q(q, 3), ring_q(q, 1), pair_q(ring_q(q, 3)), pair_q(ring_q(q, 1)), ring_q(q, 2),
            pair_q(ring_q(q, 2))]
    cols = [p, pair_p(p), ring_p(p, 3), ring_p(p, 1), pair_p(ring_p(p, 3)), pair_p(ring_p(p, 1)), ring_p(p, 2),
            pair_p(ring_p(p, 2))]
    row_next = {0: (row_pair, row_up, row_down), 1: (row_up, row_down), 2: (row_up,), 5: (row_down,)}
    col_next = {0: (col_pair, col_up, col_down), 1: (col_up, col_down), 2: (col_up,), 5: (col_down,)}

    def row_sends(i):
        slot = row_slot(rows[i])
        source = packed_ref if i == 0 else held.at[slot]
        base = 0 if i == 0 else sum(len(row_next.get(n, ())) + 1 for n in range(i))
        return [copy(base + n, source, slot, device) for n, device in enumerate(row_next.get(i, ()) + (sibling,))]

    def col_sends(i):
        slot = col_slot(cols[i])
        base = 16 + sum(len(col_next.get(n, ())) + 1 for n in range(i))
        moves = [copy(base + n, held.at[slot], slot, device) for n, device in enumerate(col_next.get(i, ()))]
        return moves, copy(base + len(moves), held.at[slot], slot, sibling), cols[i] // 4 != core

    flip = pltpu.make_async_remote_copy(
        src_ref=packed_ref, dst_ref=held.at[col_slot(q)], send_sem=send.at[15], recv_sem=arrive.at[col_slot(q)],
        device_id=flipped, device_id_type=MESH)
    stay = pltpu.make_async_copy(packed_ref, held.at[col_slot(q)], arrive.at[col_slot(q)])

    @pl.when(jnp.logical_not(diagonal))
    def _():
        flip.start()

    @pl.when(diagonal)
    def _():
        stay.start()

    for move in row_sends(0):
        move.start()
    own = pltpu.make_async_copy(packed_ref, held.at[own_slot], arrive.at[own_slot])
    own.start()

    def row_step(i):
        landed(row_slot(rows[i]))
        if i > 0:
            for move in row_sends(i):
                move.start()

    def col_step(i):
        landed(col_slot(cols[i]))
        moves, across, wanted = col_sends(i)
        for move in moves:
            move.start()

        @pl.when(wanted)
        def _():
            across.start()

    plan = {0: [(row_step, 0)], 2: [(row_step, 1), (col_step, 0)], 4: [(row_step, 2), (row_step, 3)],
            6: [(col_step, 1), (row_step, 4), (row_step, 5)], 8: [(col_step, 2), (col_step, 3)],
            10: [(row_step, 6)], 11: [(col_step, 5), (col_step, 4)], 12: [(row_step, 7)], 14: [(col_step, 6)],
            16: [(col_step, 7)]}
    unit = 2.0 ** -28 / 64.0
    scale = unit / math.sqrt(14336.0)

    def pick(values, i):
        value = values[0]
        for n in range(1, len(values)):
            value = jnp.where(i == n, values[n], value)
        return value

    def block(k, carry):
        for at, steps in plan.items():
            @pl.when(k == at)
            def _():
                for step, i in steps:
                    step(i)

        is_row = k < n_col
        place = jnp.where(is_row, k, k - n_col) // 2
        other = lax.rem(k, 2)
        part = jnp.where(other == 0, core, 1 - core)
        m = jnp.where(is_row, pick(rows, place), 4 * core + place)
        slot = jnp.where(is_row, 0, n_col) + 2 * m + part

        @pl.when(other == 1)
        def _():
            landed(slot)

        row0 = jnp.where(is_row, slot, n_col + lax.rem(slot, 8)) * EX
        form(held, slot, jnp.where(is_row, scale / 64.0, scale / 128.0), panel, row0,
             g_hi, g_lo, kin, a_work, hi_ref, lo_ref, lhs)
        return carry

    lax.fori_loop(0, n_col + 8, block, 0)

    def tile(t, carry):
        at = pl.multiple_of(t * 256, 256)
        total = None
        for k in range(4):
            term = lax.dot_general(
                panel[pl.ds(at, 256), 2048 * k:2048 * (k + 1)], panel[n_col * EX:, 2048 * k:2048 * (k + 1)],
                (((1,), (1,)), ((), ())), preferred_element_type=F32)
            total = term if total is None else total + term
        out_ref[pl.ds(at, 256), :] = total
        return carry

    lax.fori_loop(0, 4, tile, 0)

    @pl.when(jnp.logical_not(diagonal))
    def _():
        flip.wait_send()

    for i in range(chips):
        for move in row_sends(i):
            move.wait_send()
        moves, across, wanted = col_sends(i)
        for move in moves:
            move.wait_send()

        @pl.when(wanted)
        def _():
            across.wait_send()


def panels(packed, n_row, n_col):
    per = n_row
    rows, cols = n_col * EX, per * EX
    return pl.pallas_call(
        functools.partial(panel_kernel, n_row, n_col),
        out_shape=jax.ShapeDtypeStruct((rows, cols), F32),
        in_specs=[pl.BlockSpec(memory_space=pltpu.VMEM)],
        out_specs=pl.BlockSpec(memory_space=pltpu.VMEM),
        scratch_shapes=[
            pltpu.VMEM((2 * n_col, ROWS, LANE), I16),
            pltpu.VMEM((rows + cols, KO * KI), BF16),
            pltpu.VMEM((TOK, KO), BF16),
            pltpu.VMEM((TOK, KO), BF16),
            pltpu.VMEM((4, LANE, LANE), BF16),
            pltpu.VMEM((4, KI + 8, LANE), F32),
            pltpu.VMEM((8, KI, LANE), F32),
            pltpu.VMEM((8, KI, LANE), F32),
            pltpu.VMEM((8, 8 * KI, 2 * LANE), BF16),
            pltpu.SemaphoreType.DMA((32,)),
            pltpu.SemaphoreType.DMA((2 * n_col,)),
        ],
        compiler_params=pltpu.CompilerParams(
            collective_id=0, has_side_effects=True, vmem_limit_bytes=56 << 20),
        cost_estimate=pl.CostEstimate(flops=20 << 30, bytes_accessed=4 << 20, transcendentals=0),
        name="panels",
    )(packed)


def body(n_row, n_col, activations, out_grads, token_counts, proj_seeds):
    packed = project(activations, out_grads, token_counts, proj_seeds)
    return panels(packed, n_row, n_col)


def solution(mesh):
    return jax.shard_map(
        functools.partial(body, mesh.shape["row"], mesh.shape["col"]),
        mesh=mesh,
        in_specs=(P(("row", "col"), None), P(("row", "col"), None), P(("row", "col"), None), P()),
        out_specs=P("row", "col"),
        check_vma=False,
    )
```

```python
import functools
import math

import jax
import jax.numpy as jnp
from jax import lax
from jax.experimental import pallas as pl
from jax.experimental.pallas import tpu as pltpu
from jax.sharding import PartitionSpec as P

KO = 128
KI = 64
MOD = 32749
MESH = pl.DeviceIdType.MESH
F32 = jnp.float32
I32 = jnp.int32
BF16 = jnp.bfloat16
I16 = jnp.int16

TOK = 512
EX = 64
STEPS = 7
AHEAD = 2
ROWS_G = TOK
ROWS_A = ROWS_G + 4 * KI
ROWS = ROWS_A + 4 * 16
LANE = 128


def reduced(x):
    q = (x.astype(F32) * (1.0 / MOD)).astype(I32)
    return x - q * MOD


def signs_of(first, second):
    h = reduced(first * first + 5471)
    h = reduced(h * h + second)
    x = h * h + 12007
    q = (x.astype(F32) * (1.0 / MOD) + 0.5).astype(I32)
    r = x - q * MOD
    odd = (r ^ (r >> 31)) & 1
    return jnp.where(odd == 0, 1.0, -1.0).astype(F32).astype(BF16)


def centred(scalar):
    low = lax.rem(scalar, MOD)
    return jnp.where(low > MOD // 2, low - MOD, low)


def exponent(largest):
    return jnp.ceil(jnp.log2(jnp.maximum(largest, 1e-30)))


def project_kernel(seeds_ref, counts_ref, act_hbm, grad_hbm, out_ref, act, grad, g_acc, a_acc, s_a, act_sem, grad_sem):
    depth_g = grad.shape[1] // STEPS
    depth_a = act.shape[1] // 8

    def fetch_a(k):
        span = pl.ds(k * (act.shape[1] // 4), act.shape[1] // 4)
        return pltpu.make_async_copy(act_hbm.at[:, span], act.at[:, span], act_sem.at[k])

    def fetch_g(k):
        span = pl.ds(pl.multiple_of(k * depth_g, LANE), depth_g)
        return pltpu.make_async_copy(grad_hbm.at[:, span], grad.at[:, span], grad_sem.at[k])

    for k in range(AHEAD):
        fetch_g(k).start()
    g_acc[...] = jnp.zeros_like(g_acc)
    sub_a = lax.broadcasted_iota(I32, (KI, LANE), 0)
    lane_a = lax.broadcasted_iota(I32, (KI, LANE), 1)

    def part_a(k, carry):
        for part in range(depth_a // LANE):
            start = k * depth_a + part * LANE
            first = (181 * lane_a + 7 * sub_a) + centred(181 * start + seeds_ref[0])
            second = (lane_a + 31 * sub_a) + start
            s_a[:, pl.ds(pl.multiple_of(start, LANE), LANE)] = signs_of(first, second)
        return carry

    lax.fori_loop(0, 8, part_a, 0)
    sub = lax.broadcasted_iota(I32, (LANE, KO), 0)
    lane = lax.broadcasted_iota(I32, (LANE, KO), 1)

    def part_g(k, carry):
        fetch_g(k).wait()

        @pl.when(k + AHEAD < STEPS)
        def _():
            fetch_g(k + AHEAD).start()

        for n in range(4):
            @pl.when(k == n + 1)
            def _():
                fetch_a(n).start()

        signs = []
        for part in range(depth_g // LANE):
            start = k * depth_g + part * LANE
            first = (181 * sub + 7 * lane) + centred(181 * start + seeds_ref[1])
            second = (sub + 31 * lane) + start
            signs.append(signs_of(first, second))
        span = pl.ds(pl.multiple_of(k * depth_g, LANE), depth_g)
        g_acc[...] += jnp.dot(grad[:, span], jnp.concatenate(signs, axis=0), preferred_element_type=F32)
        return carry

    lax.fori_loop(0, STEPS, part_g, 0)
    for k in range(4):
        fetch_a(k).wait()
    a_acc[...] = lax.dot_general(
        s_a[...], act[...], (((1,), (1,)), ((), ())), preferred_element_type=F32
    )
    g = g_acc[...]
    a = a_acc[...]
    size = jnp.abs(g)
    g_up = exponent(jnp.max(size, axis=1, keepdims=True))
    g_across = exponent(jnp.max(size.T, axis=0, keepdims=True))
    a_up = exponent(jnp.max(jnp.abs(a), axis=0, keepdims=True))
    out_ref[0:ROWS_G, :] = jnp.round(g * jnp.exp2(14.0 - g_up)).astype(I32).astype(I16)
    a = jnp.round(a * jnp.exp2(14.0 - a_up)).astype(I32).astype(I16)
    total = g_across + a_up
    places = lax.broadcasted_iota(I32, (1, TOK), 1)

    def tally(e, carry):
        end, owner = carry
        end = end + counts_ref[0, e]
        return end, owner + (places >= end).astype(I32)

    _, owner = lax.fori_loop(0, EX, tally, (jnp.int32(0), jnp.zeros((1, TOK), I32)))
    row = lax.broadcasted_iota(I32, (16, TOK), 0)
    facts = jnp.where(row == 0, total.astype(I32), jnp.where(row == 1, owner, 0)).astype(I16)
    for k in range(4):
        out_ref[ROWS_G + KI * k:ROWS_G + KI * (k + 1), :] = a[:, LANE * k:LANE * (k + 1)]
        out_ref[ROWS_A + 16 * k:ROWS_A + 16 * (k + 1), :] = facts[:, LANE * k:LANE * (k + 1)]


def project(activations, out_grads, counts, seeds):
    depth_a = activations.shape[1]
    depth_g = out_grads.shape[1]
    return pl.pallas_call(
        project_kernel,
        out_shape=jax.ShapeDtypeStruct((ROWS, LANE), I16),
        in_specs=[
            pl.BlockSpec(memory_space=pltpu.SMEM),
            pl.BlockSpec(memory_space=pltpu.SMEM),
            pl.BlockSpec(memory_space=pl.ANY),
            pl.BlockSpec(memory_space=pl.ANY),
        ],
        out_specs=pl.BlockSpec(memory_space=pltpu.VMEM),
        scratch_shapes=[
            pltpu.VMEM((TOK, depth_a), BF16),
            pltpu.VMEM((TOK, depth_g), BF16),
            pltpu.VMEM((TOK, KO), F32),
            pltpu.VMEM((KI, TOK), F32),
            pltpu.VMEM((KI, depth_a), BF16),
            pltpu.SemaphoreType.DMA((4,)),
            pltpu.SemaphoreType.DMA((STEPS,)),
        ],
        compiler_params=pltpu.CompilerParams(vmem_limit_bytes=60 << 20),
        cost_estimate=pl.CostEstimate(flops=4 << 30, bytes_accessed=19 << 20, transcendentals=0),
        name="project",
    )(seeds, counts, activations, out_grads)


def form(held, slot, scale, target, row0, g_hi, g_lo, kin, a_work, hi_ref, lo_ref, lhs):
    g = held[slot, 0:ROWS_G, :].astype(I32).astype(F32)
    high = g.astype(BF16)
    g_hi[...] = high
    g_lo[...] = (g - high.astype(F32)).astype(BF16)
    for k in range(4):
        facts = held[slot, ROWS_A + 16 * k:ROWS_A + 16 * (k + 1), :].astype(I32)
        sizes = jnp.exp2(facts[0:1, :].astype(F32)) * scale
        part = held[slot, ROWS_G + KI * k:ROWS_G + KI * (k + 1), :].astype(I32).astype(F32)
        a_work[k, 0:KI, :] = part * sizes
        a_work[k, KI:KI + 8, :] = jnp.broadcast_to(facts[1:2, :].astype(F32), (8, LANE))
        kin[k] = jnp.broadcast_to((facts[1:2, :] >> 3).astype(F32), (LANE, LANE)).T.astype(BF16)
    sub = lax.broadcasted_iota(I32, (16, LANE), 0) & 7
    halves = []
    for group in range(8):
        low = 8 * group
        near = max(low, LANE * (group - 4)) // LANE
        far = (min(LANE * (group + 1), TOK - 8 * (7 - group)) - 1) // LANE
        a = a_work[near].reshape(KI // 8 + 1, 8, LANE)
        above, below = g_hi[LANE * near:LANE * (near + 1), :], g_lo[LANE * near:LANE * (near + 1), :]
        for k in range(near + 1, far + 1):
            owner = a_work[k, KI:KI + 8, :]
            mine = ((owner >= float(low)) & (owner < float(low + 8)))[None]
            a = jnp.where(mine, a_work[k].reshape(KI // 8 + 1, 8, LANE), a)
            mine = kin[k] == jnp.bfloat16(group)
            above = jnp.where(mine, g_hi[LANE * k:LANE * (k + 1), :], above)
            below = jnp.where(mine, g_lo[LANE * k:LANE * (k + 1), :], below)
        owner = jnp.concatenate([a[KI // 8]] * 2, axis=0)
        member = jnp.where(owner == (sub + low).astype(F32), 1.0, 0.0).astype(BF16)
        a = a[:KI // 8].reshape(KI, LANE)
        hi = a.astype(BF16).astype(F32)
        hi_ref[group] = hi
        lo_ref[group] = a - hi
        for j in range(0, KI, 2):
            for k, ref in enumerate((hi_ref, lo_ref)):
                rows = [jnp.broadcast_to(ref[group, j + n:j + n + 1, :], (8, LANE)) for n in range(2)]
                tile = jnp.concatenate(rows, axis=0).astype(BF16) * member
                lhs[group, 8 * j:8 * j + 16, LANE * k:LANE * (k + 1)] = tile
        weights = jnp.concatenate([above, below], axis=1)
        weights = jnp.concatenate([weights, weights], axis=0)
        both = jnp.dot(lhs[group], weights, preferred_element_type=F32)
        halves.append((both[:, :LANE] + both[:, LANE:]).reshape(KI, 8, LANE))
        if group % 2 == 1:
            features = jnp.concatenate(halves, axis=1).astype(BF16)
            halves = []
            at = pl.multiple_of(row0 + (group // 2) * 16, 16)
            for j in range(KI):
                target[pl.ds(at, 16), LANE * j:LANE * (j + 1)] = features[j]


def panel_kernel(n_row, n_col, packed_ref, out_ref, held, panel, g_hi, g_lo, kin, a_work, hi_ref, lo_ref, lhs,
                 send, arrive):
    p = lax.axis_index("row")
    core = lax.rem(lax.axis_index("col"), 2)
    q = lax.axis_index("col") // 2
    chips = n_col // 2
    diagonal = p == q

    def pair_q(m):
        return lax.rem(m + 4, 8)

    def ring_q(m, k):
        return (m // 4) * 4 + lax.rem(m + k, 4)

    def pair_p(m):
        return m + 1 - 2 * lax.rem(m, 2)

    def ring_p(m, k):
        return lax.rem(m + 2 * k, 8)

    sibling = (p, 2 * q + 1 - core)

    def place_of(panel, j):
        high = lax.rem(panel + j // 4 + panel // 4, 2)
        return 2 * lax.rem(panel // 2 + j - panel + 8, 4) + high

    def block_at(panel, m):
        x_lo = lax.rem(panel // 4 + panel + m, 2)
        return 4 * x_lo + lax.rem(m // 2 - panel // 2 + panel + 8, 4)

    start_place = (place_of(p, q), 2 * p + core)
    start_source = (q, 2 * block_at(q, p) + core)
    row_pair, row_up, row_down = [(p, 2 * m + core) for m in (pair_q(q), ring_q(q, 1), ring_q(q, 3))]
    col_pair, col_up, col_down = [(m, 2 * q + core) for m in (pair_p(p), ring_p(p, 1), ring_p(p, 3))]

    barrier = pltpu.get_barrier_semaphore()
    for other in (sibling, row_pair, row_up, row_down, col_pair, col_up, col_down):
        pl.semaphore_signal(barrier, inc=1, device_id=other, device_id_type=MESH)

    @pl.when(jnp.logical_not(diagonal))
    def _():
        pl.semaphore_signal(barrier, inc=1, device_id=start_source, device_id_type=MESH)

    pl.semaphore_wait(barrier, jnp.where(diagonal, 7, 8))

    def row_slot(m):
        return 2 * m + core

    def col_slot(m):
        return n_col + 2 * m + core

    def copy(number, source, slot, device):
        return pltpu.make_async_remote_copy(
            src_ref=source, dst_ref=held.at[slot], send_sem=send.at[number], recv_sem=arrive.at[slot],
            device_id=device, device_id_type=MESH)

    def landed(slot):
        copy(0, held.at[slot], slot, sibling).wait_recv()

    own_slot = row_slot(q)
    rows = [q, pair_q(q), ring_q(q, 3), ring_q(q, 1), pair_q(ring_q(q, 3)), pair_q(ring_q(q, 1)), ring_q(q, 2),
            pair_q(ring_q(q, 2))]
    cols = [p, pair_p(p), ring_p(p, 3), ring_p(p, 1), pair_p(ring_p(p, 3)), pair_p(ring_p(p, 1)), ring_p(p, 2),
            pair_p(ring_p(p, 2))]
    row_next = {0: (row_pair, row_up, row_down), 1: (row_up, row_down), 2: (row_up,), 5: (row_down,)}
    col_next = {0: (col_pair, col_up, col_down), 1: (col_up, col_down), 2: (col_up,), 5: (col_down,)}

    def row_sends(i):
        slot = row_slot(rows[i])
        source = packed_ref if i == 0 else held.at[slot]
        base = 0 if i == 0 else sum(len(row_next.get(n, ())) + 1 for n in range(i))
        return [copy(base + n, source, slot, device) for n, device in enumerate(row_next.get(i, ()) + (sibling,))]

    def col_sends(i):
        slot = col_slot(cols[i])
        base = 16 + sum(len(col_next.get(n, ())) + 1 for n in range(i))
        moves = [copy(base + n, held.at[slot], slot, device) for n, device in enumerate(col_next.get(i, ()))]
        return moves, copy(base + len(moves), held.at[slot], slot, sibling), block_at(q, cols[i]) // 4 != core

    first_slot = col_slot(place_of(p, q))
    flip = copy(15, packed_ref, first_slot, start_place)
    stay = pltpu.make_async_copy(packed_ref, held.at[first_slot], arrive.at[first_slot])

    @pl.when(jnp.logical_not(diagonal))
    def _():
        flip.start()

    @pl.when(diagonal)
    def _():
        stay.start()

    for move in row_sends(0):
        move.start()
    own = pltpu.make_async_copy(packed_ref, held.at[own_slot], arrive.at[own_slot])
    own.start()

    def row_step(i):
        landed(row_slot(rows[i]))
        if i > 0:
            for move in row_sends(i):
                move.start()

    def col_step(i):
        landed(col_slot(cols[i]))
        moves, across, wanted = col_sends(i)
        for move in moves:
            move.start()

        @pl.when(wanted)
        def _():
            across.start()

    plan = {0: [(row_step, 0)], 2: [(row_step, 1)], 3: [(col_step, 0)], 4: [(row_step, 2), (row_step, 3)],
            6: [(row_step, 4), (row_step, 5)], 8: [(col_step, 1)], 9: [(col_step, 2), (col_step, 3)],
            10: [(row_step, 6)], 12: [(row_step, 7)], 13: [(col_step, 5), (col_step, 4)], 15: [(col_step, 6)],
            20: [(col_step, 7)]}
    near = block_at(q, p) // 4 == core
    wanted_places = [jnp.where(near, cols[a], cols[b]) for a, b in ((0, 1), (2, 4), (3, 5), (6, 7))]
    unit = 2.0 ** -28 / 64.0
    scale = unit / math.sqrt(14336.0)

    def pick(values, i):
        value = values[0]
        for n in range(1, len(values)):
            value = jnp.where(i == n, values[n], value)
        return value

    def half(n):
        low = n_col * EX + 256 * n
        offsets = [pl.multiple_of(lax.rem(block_at(q, m), 4) * 128, 128) for m in wanted_places[2 * n:2 * n + 2]]

        def tile(t, carry):
            at = pl.multiple_of(t * 256, 256)
            total = None
            for k in range(4):
                term = lax.dot_general(
                    panel[pl.ds(at, 256), 2048 * k:2048 * (k + 1)], panel[low:low + 256, 2048 * k:2048 * (k + 1)],
                    (((1,), (1,)), ((), ())), preferred_element_type=F32)
                total = term if total is None else total + term
            for i in range(2):
                out_ref[pl.ds(at, 256), pl.ds(offsets[i], 128)] = total[:, 128 * i:128 * (i + 1)]
            return carry

        lax.fori_loop(0, 4, tile, 0)

    def block(k, carry):
        @pl.when(k == n_col + 4)
        def _():
            half(0)

        for at, steps in plan.items():
            @pl.when(k == at)
            def _():
                for step, i in steps:
                    step(i)

        is_row = k < n_col
        place = jnp.where(is_row, k, k - n_col) // 2
        other = lax.rem(k, 2)
        part = jnp.where(other == 0, core, 1 - core)
        m = jnp.where(is_row, pick(rows, place), pick(wanted_places, place))
        slot = jnp.where(is_row, 0, n_col) + 2 * m + part

        @pl.when(other == 1)
        def _():
            landed(slot)

        row0 = jnp.where(is_row, slot, n_col + 2 * place + part) * EX
        form(held, slot, jnp.where(is_row, scale / 64.0, scale / 128.0), panel, row0,
             g_hi, g_lo, kin, a_work, hi_ref, lo_ref, lhs)
        return carry

    lax.fori_loop(0, n_col + 8, block, 0)
    half(1)

    @pl.when(jnp.logical_not(diagonal))
    def _():
        flip.wait_send()

    for i in range(chips):
        for move in row_sends(i):
            move.wait_send()
        moves, across, wanted = col_sends(i)
        for move in moves:
            move.wait_send()

        @pl.when(wanted)
        def _():
            across.wait_send()


def panels(packed, n_row, n_col):
    per = n_row
    rows, cols = n_col * EX, per * EX
    return pl.pallas_call(
        functools.partial(panel_kernel, n_row, n_col),
        out_shape=jax.ShapeDtypeStruct((rows, cols), F32),
        in_specs=[pl.BlockSpec(memory_space=pltpu.VMEM)],
        out_specs=pl.BlockSpec(memory_space=pltpu.VMEM),
        scratch_shapes=[
            pltpu.VMEM((2 * n_col, ROWS, LANE), I16),
            pltpu.VMEM((rows + cols, KO * KI), BF16),
            pltpu.VMEM((TOK, KO), BF16),
            pltpu.VMEM((TOK, KO), BF16),
            pltpu.VMEM((4, LANE, LANE), BF16),
            pltpu.VMEM((4, KI + 8, LANE), F32),
            pltpu.VMEM((8, KI, LANE), F32),
            pltpu.VMEM((8, KI, LANE), F32),
            pltpu.VMEM((8, 8 * KI, 2 * LANE), BF16),
            pltpu.SemaphoreType.DMA((32,)),
            pltpu.SemaphoreType.DMA((2 * n_col,)),
        ],
        compiler_params=pltpu.CompilerParams(
            collective_id=0, has_side_effects=True, vmem_limit_bytes=56 << 20),
        cost_estimate=pl.CostEstimate(flops=20 << 30, bytes_accessed=4 << 20, transcendentals=0),
        name="panels",
    )(packed)


def body(n_row, n_col, activations, out_grads, token_counts, proj_seeds):
    packed = project(activations, out_grads, token_counts, proj_seeds)
    return panels(packed, n_row, n_col)


def solution(mesh):
    return jax.shard_map(
        functools.partial(body, mesh.shape["row"], mesh.shape["col"]),
        mesh=mesh,
        in_specs=(P(("row", "col"), None), P(("row", "col"), None), P(("row", "col"), None), P()),
        out_specs=P("row", "col"),
        check_vma=False,
    )
```

```python
import functools
import math

import jax
import jax.numpy as jnp
from jax import lax
from jax.experimental import pallas as pl
from jax.experimental.pallas import tpu as pltpu
from jax.sharding import PartitionSpec as P

KO = 128
KI = 64
MOD = 32749
MESH = pl.DeviceIdType.MESH
F32 = jnp.float32
I32 = jnp.int32
BF16 = jnp.bfloat16
I16 = jnp.int16

TOK = 512
EX = 64
STEPS = 7
AHEAD = 2
ROWS_G = TOK
ROWS_A = ROWS_G + 4 * KI
ROWS = ROWS_A + 16
LANE = 128


def reduced(x):
    q = (x.astype(F32) * (1.0 / MOD)).astype(I32)
    return x - q * MOD


def signs_of(first, second):
    h = reduced(first * first + 5471)
    h = reduced(h * h + second)
    x = h * h + 12007
    q = (x.astype(F32) * (1.0 / MOD) + 0.5).astype(I32)
    r = x - q * MOD
    odd = (r ^ (r >> 31)) & 1
    return jnp.where(odd == 0, 1.0, -1.0).astype(F32).astype(BF16)


def centred(scalar):
    low = lax.rem(scalar, MOD)
    return jnp.where(low > MOD // 2, low - MOD, low)


def exponent(largest):
    return jnp.ceil(jnp.log2(jnp.maximum(largest, 1e-30)))


def project_kernel(seeds_ref, counts_ref, act_hbm, grad_hbm, out_ref, act, grad, g_acc, a_acc, s_a, act_sem, grad_sem):
    depth_g = grad.shape[1] // STEPS
    depth_a = act.shape[1] // 8

    def fetch_a(k):
        span = pl.ds(k * (act.shape[1] // 4), act.shape[1] // 4)
        return pltpu.make_async_copy(act_hbm.at[:, span], act.at[:, span], act_sem.at[k])

    def fetch_g(k):
        span = pl.ds(pl.multiple_of(k * depth_g, LANE), depth_g)
        return pltpu.make_async_copy(grad_hbm.at[:, span], grad.at[:, span], grad_sem.at[k])

    for k in range(AHEAD):
        fetch_g(k).start()
    g_acc[...] = jnp.zeros_like(g_acc)
    sub_a = lax.broadcasted_iota(I32, (KI, LANE), 0)
    lane_a = lax.broadcasted_iota(I32, (KI, LANE), 1)

    def part_a(k, carry):
        for part in range(depth_a // LANE):
            start = k * depth_a + part * LANE
            first = (181 * lane_a + 7 * sub_a) + centred(181 * start + seeds_ref[0])
            second = (lane_a + 31 * sub_a) + start
            s_a[:, pl.ds(pl.multiple_of(start, LANE), LANE)] = signs_of(first, second)
        return carry

    lax.fori_loop(0, 8, part_a, 0)
    sub = lax.broadcasted_iota(I32, (LANE, KO), 0)
    lane = lax.broadcasted_iota(I32, (LANE, KO), 1)

    def part_g(k, carry):
        fetch_g(k).wait()

        @pl.when(k + AHEAD < STEPS)
        def _():
            fetch_g(k + AHEAD).start()

        for n in range(4):
            @pl.when(k == n + 1)
            def _():
                fetch_a(n).start()

        signs = []
        for part in range(depth_g // LANE):
            start = k * depth_g + part * LANE
            first = (181 * sub + 7 * lane) + centred(181 * start + seeds_ref[1])
            second = (sub + 31 * lane) + start
            signs.append(signs_of(first, second))
        span = pl.ds(pl.multiple_of(k * depth_g, LANE), depth_g)
        g_acc[...] += jnp.dot(grad[:, span], jnp.concatenate(signs, axis=0), preferred_element_type=F32)
        return carry

    lax.fori_loop(0, STEPS, part_g, 0)
    for k in range(4):
        fetch_a(k).wait()
    a_acc[...] = lax.dot_general(
        s_a[...], act[...], (((1,), (1,)), ((), ())), preferred_element_type=F32
    )
    g = g_acc[...]
    a = a_acc[...]
    size = jnp.abs(g)
    g_up = exponent(jnp.max(size, axis=1, keepdims=True))
    g_across = exponent(jnp.max(size.T, axis=0, keepdims=True))
    a_up = exponent(jnp.max(jnp.abs(a), axis=0, keepdims=True))
    out_ref[0:ROWS_G, :] = jnp.round(g * jnp.exp2(14.0 - g_up)).astype(I32).astype(I16)
    a = jnp.round(a * jnp.exp2(14.0 - a_up)).astype(I32).astype(I16)
    total = g_across + a_up
    places = lax.broadcasted_iota(I32, (1, TOK), 1)

    def tally(e, carry):
        end, owner = carry
        end = end + counts_ref[0, e]
        return end, owner + (places >= end).astype(I32)

    _, owner = lax.fori_loop(0, EX, tally, (jnp.int32(0), jnp.zeros((1, TOK), I32)))
    facts = [total.astype(I32)[:, LANE * k:LANE * (k + 1)] for k in range(4)]
    facts += [owner[:, LANE * k:LANE * (k + 1)] for k in range(4)]
    out_ref[ROWS_A:, :] = jnp.concatenate(facts + [jnp.zeros((8, LANE), I32)], axis=0).astype(I16)
    for k in range(4):
        out_ref[ROWS_G + KI * k:ROWS_G + KI * (k + 1), :] = a[:, LANE * k:LANE * (k + 1)]


def project(activations, out_grads, counts, seeds):
    depth_a = activations.shape[1]
    depth_g = out_grads.shape[1]
    return pl.pallas_call(
        project_kernel,
        out_shape=jax.ShapeDtypeStruct((ROWS, LANE), I16),
        in_specs=[
            pl.BlockSpec(memory_space=pltpu.SMEM),
            pl.BlockSpec(memory_space=pltpu.SMEM),
            pl.BlockSpec(memory_space=pl.ANY),
            pl.BlockSpec(memory_space=pl.ANY),
        ],
        out_specs=pl.BlockSpec(memory_space=pltpu.VMEM),
        scratch_shapes=[
            pltpu.VMEM((TOK, depth_a), BF16),
            pltpu.VMEM((TOK, depth_g), BF16),
            pltpu.VMEM((TOK, KO), F32),
            pltpu.VMEM((KI, TOK), F32),
            pltpu.VMEM((KI, depth_a), BF16),
            pltpu.SemaphoreType.DMA((4,)),
            pltpu.SemaphoreType.DMA((STEPS,)),
        ],
        compiler_params=pltpu.CompilerParams(vmem_limit_bytes=60 << 20),
        cost_estimate=pl.CostEstimate(flops=4 << 30, bytes_accessed=19 << 20, transcendentals=0),
        name="project",
    )(seeds, counts, activations, out_grads)


def form(held, slot, scale, target, row0, g_hi, g_lo, kin, a_work, hi_ref, lo_ref, lhs):
    g = held[slot, 0:ROWS_G, :].astype(I32).astype(F32)
    high = g.astype(BF16)
    g_hi[...] = high
    g_lo[...] = (g - high.astype(F32)).astype(BF16)
    facts = held[slot, ROWS_A:, :].astype(I32)
    for k in range(4):
        sizes = jnp.exp2(facts[k:k + 1, :].astype(F32)) * scale
        owner = facts[4 + k:5 + k, :]
        part = held[slot, ROWS_G + KI * k:ROWS_G + KI * (k + 1), :].astype(I32).astype(F32)
        a_work[k, 0:KI, :] = part * sizes
        a_work[k, KI:KI + 8, :] = jnp.broadcast_to(owner.astype(F32), (8, LANE))
        kin[k] = jnp.broadcast_to((owner >> 3).astype(F32), (LANE, LANE)).T.astype(BF16)
    sub = lax.broadcasted_iota(I32, (16, LANE), 0) & 7
    halves = []
    for group in range(8):
        low = 8 * group
        near = max(low, LANE * (group - 4)) // LANE
        far = (min(LANE * (group + 1), TOK - 8 * (7 - group)) - 1) // LANE
        a = a_work[near].reshape(KI // 8 + 1, 8, LANE)
        above, below = g_hi[LANE * near:LANE * (near + 1), :], g_lo[LANE * near:LANE * (near + 1), :]
        for k in range(near + 1, far + 1):
            owner = a_work[k, KI:KI + 8, :]
            mine = ((owner >= float(low)) & (owner < float(low + 8)))[None]
            a = jnp.where(mine, a_work[k].reshape(KI // 8 + 1, 8, LANE), a)
            mine = kin[k] == jnp.bfloat16(group)
            above = jnp.where(mine, g_hi[LANE * k:LANE * (k + 1), :], above)
            below = jnp.where(mine, g_lo[LANE * k:LANE * (k + 1), :], below)
        owner = jnp.concatenate([a[KI // 8]] * 2, axis=0)
        member = jnp.where(owner == (sub + low).astype(F32), 1.0, 0.0).astype(BF16)
        a = a[:KI // 8].reshape(KI, LANE)
        hi = a.astype(BF16).astype(F32)
        hi_ref[group] = hi
        lo_ref[group] = a - hi
        for j in range(0, KI, 2):
            for k, ref in enumerate((hi_ref, lo_ref)):
                rows = [jnp.broadcast_to(ref[group, j + n:j + n + 1, :], (8, LANE)) for n in range(2)]
                tile = jnp.concatenate(rows, axis=0).astype(BF16) * member
                lhs[group, 8 * j:8 * j + 16, LANE * k:LANE * (k + 1)] = tile
        weights = jnp.concatenate([above, below], axis=1)
        weights = jnp.concatenate([weights, weights], axis=0)
        both = jnp.dot(lhs[group], weights, preferred_element_type=F32)
        halves.append((both[:, :LANE] + both[:, LANE:]).reshape(KI, 8, LANE))
        if group % 2 == 1:
            features = jnp.concatenate(halves, axis=1).astype(BF16)
            halves = []
            at = pl.multiple_of(row0 + (group // 2) * 16, 16)
            for j in range(KI):
                target[pl.ds(at, 16), LANE * j:LANE * (j + 1)] = features[j]


def panel_kernel(n_row, n_col, packed_ref, out_ref, held, panel, g_hi, g_lo, kin, a_work, hi_ref, lo_ref, lhs,
                 send, arrive):
    p = lax.axis_index("row")
    core = lax.rem(lax.axis_index("col"), 2)
    q = lax.axis_index("col") // 2
    chips = n_col // 2

    def pair_q(m):
        return lax.rem(m + 4, 8)

    def ring_q(m, k):
        return (m // 4) * 4 + lax.rem(m + k, 4)

    def pair_p(m):
        return m + 1 - 2 * lax.rem(m, 2)

    def ring_p(m, k):
        return lax.rem(m + 2 * k, 8)

    sibling = (p, 2 * q + 1 - core)

    def place_of(panel, j):
        high = lax.rem(panel + j // 4 + panel // 4, 2)
        return 2 * lax.rem(panel // 2 + 2 + panel - j + 8, 4) + high

    def block_at(panel, m):
        x_lo = lax.rem(panel // 4 + panel + m, 2)
        return 4 * x_lo + lax.rem(panel + 2 + panel // 2 - m // 2 + 8, 4)

    start_place = (place_of(p, q), 2 * p + core)
    start_source = (q, 2 * block_at(q, p) + core)
    row_pair, row_up, row_down = [(p, 2 * m + core) for m in (pair_q(q), ring_q(q, 1), ring_q(q, 3))]
    col_pair, col_up, col_down = [(m, 2 * q + core) for m in (pair_p(p), ring_p(p, 1), ring_p(p, 3))]

    barrier = pltpu.get_barrier_semaphore()
    for other in (sibling, row_pair, row_up, row_down, col_pair, col_up, col_down):
        pl.semaphore_signal(barrier, inc=1, device_id=other, device_id_type=MESH)

    pl.semaphore_signal(barrier, inc=1, device_id=start_source, device_id_type=MESH)
    pl.semaphore_wait(barrier, 8)

    def row_slot(m):
        return 2 * m + core

    def col_slot(m):
        return n_col + 2 * m + core

    def copy(number, source, slot, device):
        return pltpu.make_async_remote_copy(
            src_ref=source, dst_ref=held.at[slot], send_sem=send.at[number], recv_sem=arrive.at[slot],
            device_id=device, device_id_type=MESH)

    def landed(slot):
        copy(0, held.at[slot], slot, sibling).wait_recv()

    own_slot = row_slot(q)
    rows = [q, pair_q(q), ring_q(q, 3), ring_q(q, 1), pair_q(ring_q(q, 3)), pair_q(ring_q(q, 1)), ring_q(q, 2),
            pair_q(ring_q(q, 2))]
    cols = [p, pair_p(p), ring_p(p, 3), ring_p(p, 1), pair_p(ring_p(p, 3)), pair_p(ring_p(p, 1)), ring_p(p, 2),
            pair_p(ring_p(p, 2))]
    row_next = {0: (row_pair, row_up, row_down), 1: (row_up, row_down), 2: (row_up,), 5: (row_down,)}
    col_next = {0: (col_pair, col_up, col_down), 1: (col_up, col_down), 2: (col_up,), 5: (col_down,)}

    def row_sends(i):
        slot = row_slot(rows[i])
        source = packed_ref if i == 0 else held.at[slot]
        base = 0 if i == 0 else sum(len(row_next.get(n, ())) + 1 for n in range(i))
        return [copy(base + n, source, slot, device) for n, device in enumerate(row_next.get(i, ()) + (sibling,))]

    def col_sends(i):
        slot = col_slot(cols[i])
        base = 16 + sum(len(col_next.get(n, ())) + 1 for n in range(i))
        moves = [copy(base + n, held.at[slot], slot, device) for n, device in enumerate(col_next.get(i, ()))]
        return moves, copy(base + len(moves), held.at[slot], slot, sibling), block_at(q, cols[i]) // 4 != core

    first_slot = col_slot(place_of(p, q))
    flip = copy(15, packed_ref, first_slot, start_place)
    flip.start()

    for move in row_sends(0):
        move.start()
    own = pltpu.make_async_copy(packed_ref, held.at[own_slot], arrive.at[own_slot])
    own.start()

    def row_step(i):
        landed(row_slot(rows[i]))
        if i > 0:
            for move in row_sends(i):
                move.start()

    def col_step(i):
        landed(col_slot(cols[i]))
        moves, across, wanted = col_sends(i)
        for move in moves:
            move.start()

        @pl.when(wanted)
        def _():
            across.start()

    plan = {0: [(row_step, 0)], 2: [(row_step, 1)], 3: [(col_step, 0)], 4: [(row_step, 2), (row_step, 3)],
            6: [(row_step, 4), (row_step, 5)], 8: [(col_step, 1)], 9: [(col_step, 2), (col_step, 3)],
            10: [(row_step, 6)], 12: [(row_step, 7)], 13: [(col_step, 5), (col_step, 4)], 15: [(col_step, 6)],
            20: [(col_step, 7)]}
    near = block_at(q, p) // 4 == core
    wanted_places = [jnp.where(near, cols[a], cols[b]) for a, b in ((0, 1), (2, 4), (3, 5), (6, 7))]
    unit = 2.0 ** -28 / 64.0
    scale = unit / math.sqrt(14336.0)

    def pick(values, i):
        value = values[0]
        for n in range(1, len(values)):
            value = jnp.where(i == n, values[n], value)
        return value

    def half(n):
        low = n_col * EX + 256 * n
        offsets = [pl.multiple_of(lax.rem(block_at(q, m), 4) * 128, 128) for m in wanted_places[2 * n:2 * n + 2]]

        def tile(t, carry):
            at = pl.multiple_of(t * 256, 256)
            total = None
            for k in range(4):
                term = lax.dot_general(
                    panel[pl.ds(at, 256), 2048 * k:2048 * (k + 1)], panel[low:low + 256, 2048 * k:2048 * (k + 1)],
                    (((1,), (1,)), ((), ())), preferred_element_type=F32)
                total = term if total is None else total + term
            for i in range(2):
                out_ref[pl.ds(at, 256), pl.ds(offsets[i], 128)] = total[:, 128 * i:128 * (i + 1)]
            return carry

        lax.fori_loop(0, 4, tile, 0)

    def block(k, carry):
        @pl.when(k == n_col + 4)
        def _():
            half(0)

        for at, steps in plan.items():
            @pl.when(k == at)
            def _():
                for step, i in steps:
                    step(i)

        is_row = k < n_col
        place = jnp.where(is_row, k, k - n_col) // 2
        other = lax.rem(k, 2)
        part = jnp.where(other == 0, core, 1 - core)
        m = jnp.where(is_row, pick(rows, place), pick(wanted_places, place))
        slot = jnp.where(is_row, 0, n_col) + 2 * m + part

        @pl.when(other == 1)
        def _():
            landed(slot)

        row0 = jnp.where(is_row, slot, n_col + 2 * place + part) * EX
        form(held, slot, jnp.where(is_row, scale / 64.0, scale / 128.0), panel, row0,
             g_hi, g_lo, kin, a_work, hi_ref, lo_ref, lhs)
        return carry

    lax.fori_loop(0, n_col + 8, block, 0)
    half(1)

    flip.wait_send()

    for i in range(chips):
        for move in row_sends(i):
            move.wait_send()
        moves, across, wanted = col_sends(i)
        for move in moves:
            move.wait_send()

        @pl.when(wanted)
        def _():
            across.wait_send()


def panels(packed, n_row, n_col):
    per = n_row
    rows, cols = n_col * EX, per * EX
    return pl.pallas_call(
        functools.partial(panel_kernel, n_row, n_col),
        out_shape=jax.ShapeDtypeStruct((rows, cols), F32),
        in_specs=[pl.BlockSpec(memory_space=pltpu.VMEM)],
        out_specs=pl.BlockSpec(memory_space=pltpu.VMEM),
        scratch_shapes=[
            pltpu.VMEM((2 * n_col, ROWS, LANE), I16),
            pltpu.VMEM((rows + cols, KO * KI), BF16),
            pltpu.VMEM((TOK, KO), BF16),
            pltpu.VMEM((TOK, KO), BF16),
            pltpu.VMEM((4, LANE, LANE), BF16),
            pltpu.VMEM((4, KI + 8, LANE), F32),
            pltpu.VMEM((8, KI, LANE), F32),
            pltpu.VMEM((8, KI, LANE), F32),
            pltpu.VMEM((8, 8 * KI, 2 * LANE), BF16),
            pltpu.SemaphoreType.DMA((32,)),
            pltpu.SemaphoreType.DMA((2 * n_col,)),
        ],
        compiler_params=pltpu.CompilerParams(
            collective_id=0, has_side_effects=True, vmem_limit_bytes=56 << 20),
        cost_estimate=pl.CostEstimate(flops=20 << 30, bytes_accessed=4 << 20, transcendentals=0),
        name="panels",
    )(packed)


def body(n_row, n_col, activations, out_grads, token_counts, proj_seeds):
    packed = project(activations, out_grads, token_counts, proj_seeds)
    return panels(packed, n_row, n_col)


def solution(mesh):
    return jax.shard_map(
        functools.partial(body, mesh.shape["row"], mesh.shape["col"]),
        mesh=mesh,
        in_specs=(P(("row", "col"), None), P(("row", "col"), None), P(("row", "col"), None), P()),
        out_specs=P("row", "col"),
        check_vma=False,
    )
```

```python
import functools
import math

import jax
import jax.numpy as jnp
from jax import lax
from jax.experimental import pallas as pl
from jax.experimental.pallas import tpu as pltpu
from jax.sharding import PartitionSpec as P

KO = 128
KI = 64
MOD = 32749
MESH = pl.DeviceIdType.MESH
F32 = jnp.float32
I32 = jnp.int32
BF16 = jnp.bfloat16
I16 = jnp.int16

TOK = 512
EX = 64
STEPS = 7
AHEAD = 2
ROWS_G = TOK
ROWS_A = ROWS_G + 4 * KI
ROWS = ROWS_A + 16
LANE = 128


def reduced(x):
    q = (x.astype(F32) * (1.0 / MOD)).astype(I32)
    return x - q * MOD


def signs_of(first, second):
    h = reduced(first * first + 5471)
    h = reduced(h * h + second)
    x = h * h + 12007
    q = (x.astype(F32) * (1.0 / MOD) + 0.5).astype(I32)
    r = x - q * MOD
    odd = (r ^ (r >> 31)) & 1
    return jnp.where(odd == 0, 1.0, -1.0).astype(F32).astype(BF16)


def centred(scalar):
    low = lax.rem(scalar, MOD)
    return jnp.where(low > MOD // 2, low - MOD, low)


def exponent(largest):
    return jnp.ceil(jnp.log2(jnp.maximum(largest, 1e-30)))


def project_kernel(seeds_ref, counts_ref, act_hbm, grad_hbm, out_ref, act, grad, g_acc, a_acc, s_a, act_sem, grad_sem):
    depth_g = grad.shape[1] // STEPS
    depth_a = act.shape[1] // 8

    def fetch_a(k):
        span = pl.ds(k * (act.shape[1] // 4), act.shape[1] // 4)
        return pltpu.make_async_copy(act_hbm.at[:, span], act.at[:, span], act_sem.at[k])

    def fetch_g(k):
        span = pl.ds(pl.multiple_of(k * depth_g, LANE), depth_g)
        return pltpu.make_async_copy(grad_hbm.at[:, span], grad.at[:, span], grad_sem.at[k])

    for k in range(AHEAD):
        fetch_g(k).start()
    g_acc[...] = jnp.zeros_like(g_acc)
    sub_a = lax.broadcasted_iota(I32, (KI, LANE), 0)
    lane_a = lax.broadcasted_iota(I32, (KI, LANE), 1)

    def part_a(k, carry):
        for part in range(depth_a // LANE):
            start = k * depth_a + part * LANE
            first = (181 * lane_a + 7 * sub_a) + centred(181 * start + seeds_ref[0])
            second = (lane_a + 31 * sub_a) + start
            s_a[:, pl.ds(pl.multiple_of(start, LANE), LANE)] = signs_of(first, second)
        return carry

    lax.fori_loop(0, 8, part_a, 0)
    sub = lax.broadcasted_iota(I32, (LANE, KO), 0)
    lane = lax.broadcasted_iota(I32, (LANE, KO), 1)

    def part_g(k, carry):
        fetch_g(k).wait()

        @pl.when(k + AHEAD < STEPS)
        def _():
            fetch_g(k + AHEAD).start()

        for n in range(4):
            @pl.when(k == n + 1)
            def _():
                fetch_a(n).start()

        signs = []
        for part in range(depth_g // LANE):
            start = k * depth_g + part * LANE
            first = (181 * sub + 7 * lane) + centred(181 * start + seeds_ref[1])
            second = (sub + 31 * lane) + start
            signs.append(signs_of(first, second))
        span = pl.ds(pl.multiple_of(k * depth_g, LANE), depth_g)
        g_acc[...] += jnp.dot(grad[:, span], jnp.concatenate(signs, axis=0), preferred_element_type=F32)
        return carry

    lax.fori_loop(0, STEPS, part_g, 0)
    for k in range(4):
        fetch_a(k).wait()
    a_acc[...] = lax.dot_general(
        s_a[...], act[...], (((1,), (1,)), ((), ())), preferred_element_type=F32
    )
    g = g_acc[...]
    a = a_acc[...]
    size = jnp.abs(g)
    g_up = exponent(jnp.max(size, axis=1, keepdims=True))
    g_across = exponent(jnp.max(size.T, axis=0, keepdims=True))
    a_up = exponent(jnp.max(jnp.abs(a), axis=0, keepdims=True))
    out_ref[0:ROWS_G, :] = jnp.round(g * jnp.exp2(14.0 - g_up)).astype(I32).astype(I16)
    a = jnp.round(a * jnp.exp2(14.0 - a_up)).astype(I32).astype(I16)
    total = g_across + a_up
    places = lax.broadcasted_iota(I32, (1, TOK), 1)

    def tally(e, carry):
        end, owner = carry
        end = end + counts_ref[0, e]
        return end, owner + (places >= end).astype(I32)

    _, owner = lax.fori_loop(0, EX, tally, (jnp.int32(0), jnp.zeros((1, TOK), I32)))
    facts = [total.astype(I32)[:, LANE * k:LANE * (k + 1)] for k in range(4)]
    facts += [owner[:, LANE * k:LANE * (k + 1)] for k in range(4)]
    out_ref[ROWS_A:, :] = jnp.concatenate(facts + [jnp.zeros((8, LANE), I32)], axis=0).astype(I16)
    for k in range(4):
        out_ref[ROWS_G + KI * k:ROWS_G + KI * (k + 1), :] = a[:, LANE * k:LANE * (k + 1)]


def project(activations, out_grads, counts, seeds):
    depth_a = activations.shape[1]
    depth_g = out_grads.shape[1]
    return pl.pallas_call(
        project_kernel,
        out_shape=jax.ShapeDtypeStruct((ROWS, LANE), I16),
        in_specs=[
            pl.BlockSpec(memory_space=pltpu.SMEM),
            pl.BlockSpec(memory_space=pltpu.SMEM),
            pl.BlockSpec(memory_space=pl.ANY),
            pl.BlockSpec(memory_space=pl.ANY),
        ],
        out_specs=pl.BlockSpec(memory_space=pltpu.VMEM),
        scratch_shapes=[
            pltpu.VMEM((TOK, depth_a), BF16),
            pltpu.VMEM((TOK, depth_g), BF16),
            pltpu.VMEM((TOK, KO), F32),
            pltpu.VMEM((KI, TOK), F32),
            pltpu.VMEM((KI, depth_a), BF16),
            pltpu.SemaphoreType.DMA((4,)),
            pltpu.SemaphoreType.DMA((STEPS,)),
        ],
        compiler_params=pltpu.CompilerParams(vmem_limit_bytes=60 << 20),
        cost_estimate=pl.CostEstimate(flops=4 << 30, bytes_accessed=19 << 20, transcendentals=0),
        name="project",
    )(seeds, counts, activations, out_grads)


def form(held, slot, scale, target, row0, g_hi, g_lo, kin, a_work, hi_ref, lo_ref, lhs):
    g = held[slot, 0:ROWS_G, :].astype(I32).astype(F32)
    high = g.astype(BF16)
    g_hi[...] = high
    g_lo[...] = (g - high.astype(F32)).astype(BF16)
    facts = held[slot, ROWS_A:, :].astype(I32)
    for k in range(4):
        sizes = jnp.exp2(facts[k:k + 1, :].astype(F32)) * scale
        owner = facts[4 + k:5 + k, :]
        part = held[slot, ROWS_G + KI * k:ROWS_G + KI * (k + 1), :].astype(I32).astype(F32)
        a_work[k, 0:KI, :] = part * sizes
        a_work[k, KI:KI + 8, :] = jnp.broadcast_to(owner.astype(F32), (8, LANE))
        kin[k] = jnp.broadcast_to((owner >> 3).astype(F32), (LANE, LANE)).T.astype(BF16)
    sub = lax.broadcasted_iota(I32, (16, LANE), 0) & 7
    halves = []
    for group in range(8):
        low = 8 * group
        near = max(low, LANE * (group - 4)) // LANE
        far = (min(LANE * (group + 1), TOK - 8 * (7 - group)) - 1) // LANE
        a = a_work[near].reshape(KI // 8 + 1, 8, LANE)
        above, below = g_hi[LANE * near:LANE * (near + 1), :], g_lo[LANE * near:LANE * (near + 1), :]
        for k in range(near + 1, far + 1):
            owner = a_work[k, KI:KI + 8, :]
            mine = ((owner >= float(low)) & (owner < float(low + 8)))[None]
            a = jnp.where(mine, a_work[k].reshape(KI // 8 + 1, 8, LANE), a)
            mine = kin[k] == jnp.bfloat16(group)
            above = jnp.where(mine, g_hi[LANE * k:LANE * (k + 1), :], above)
            below = jnp.where(mine, g_lo[LANE * k:LANE * (k + 1), :], below)
        owner = jnp.concatenate([a[KI // 8]] * 2, axis=0)
        member = jnp.where(owner == (sub + low).astype(F32), 1.0, 0.0).astype(BF16)
        a = a[:KI // 8].reshape(KI, LANE)
        hi = a.astype(BF16).astype(F32)
        hi_ref[group] = hi
        lo_ref[group] = a - hi
        for j in range(0, KI, 2):
            for k, ref in enumerate((hi_ref, lo_ref)):
                rows = [jnp.broadcast_to(ref[group, j + n:j + n + 1, :], (8, LANE)) for n in range(2)]
                tile = jnp.concatenate(rows, axis=0).astype(BF16) * member
                lhs[group, 8 * j:8 * j + 16, LANE * k:LANE * (k + 1)] = tile
        weights = jnp.concatenate([above, below], axis=1)
        weights = jnp.concatenate([weights, weights], axis=0)
        both = jnp.dot(lhs[group], weights, preferred_element_type=F32)
        halves.append((both[:, :LANE] + both[:, LANE:]).reshape(KI, 8, LANE))
        if group % 2 == 1:
            features = jnp.concatenate(halves, axis=1).astype(BF16)
            halves = []
            at = pl.multiple_of(row0 + (group // 2) * 16, 16)
            for j in range(KI):
                target[pl.ds(at, 16), LANE * j:LANE * (j + 1)] = features[j]


def panel_kernel(n_row, n_col, packed_ref, out_ref, held, panel, g_hi, g_lo, kin, a_work, hi_ref, lo_ref, lhs,
                 send, arrive):
    p = lax.axis_index("row")
    core = lax.rem(lax.axis_index("col"), 2)
    q = lax.axis_index("col") // 2
    chips = n_col // 2

    def pair_q(m):
        return lax.rem(m + 4, 8)

    def ring_q(m, k):
        return (m // 4) * 4 + lax.rem(m + k, 4)

    def pair_p(m):
        return m + 1 - 2 * lax.rem(m, 2)

    def ring_p(m, k):
        return lax.rem(m + 2 * k, 8)

    sibling = (p, 2 * q + 1 - core)

    def place_of(panel, j):
        high = lax.rem(panel + j // 4 + panel // 4, 2)
        return 2 * lax.rem(panel // 2 + 2 + panel - j + 8, 4) + high

    def block_at(panel, m):
        x_lo = lax.rem(panel // 4 + panel + m, 2)
        return 4 * x_lo + lax.rem(panel + 2 + panel // 2 - m // 2 + 8, 4)

    start_place = (place_of(p, q), 2 * p + core)
    start_source = (q, 2 * block_at(q, p) + core)
    row_pair, row_up, row_down = [(p, 2 * m + core) for m in (pair_q(q), ring_q(q, 1), ring_q(q, 3))]
    col_pair, col_up, col_down = [(m, 2 * q + core) for m in (pair_p(p), ring_p(p, 1), ring_p(p, 3))]

    barrier = pltpu.get_barrier_semaphore()
    for other in (sibling, row_pair, row_up, row_down, col_pair, col_up, col_down):
        pl.semaphore_signal(barrier, inc=1, device_id=other, device_id_type=MESH)

    pl.semaphore_signal(barrier, inc=1, device_id=start_source, device_id_type=MESH)
    pl.semaphore_wait(barrier, 8)

    def row_slot(m):
        return 2 * m + core

    def col_slot(m):
        return n_col + 2 * m + core

    def copy(number, source, slot, device):
        return pltpu.make_async_remote_copy(
            src_ref=source, dst_ref=held.at[slot], send_sem=send.at[number], recv_sem=arrive.at[slot],
            device_id=device, device_id_type=MESH)

    def landed(slot):
        copy(0, held.at[slot], slot, sibling).wait_recv()

    own_slot = row_slot(q)
    rows = [q, pair_q(q), ring_q(q, 3), ring_q(q, 1), pair_q(ring_q(q, 3)), pair_q(ring_q(q, 1)), ring_q(q, 2),
            pair_q(ring_q(q, 2))]
    cols = [p, pair_p(p), ring_p(p, 3), ring_p(p, 1), pair_p(ring_p(p, 3)), pair_p(ring_p(p, 1)), ring_p(p, 2),
            pair_p(ring_p(p, 2))]
    row_next = {0: (row_pair, row_up, row_down), 1: (row_up, row_down), 2: (row_up,), 5: (row_down,)}
    col_next = {0: (col_pair, col_up, col_down), 1: (col_up, col_down), 2: (col_up,), 5: (col_down,)}

    def row_sends(i):
        slot = row_slot(rows[i])
        source = packed_ref if i == 0 else held.at[slot]
        base = 0 if i == 0 else sum(len(row_next.get(n, ())) + 1 for n in range(i))
        return [copy(base + n, source, slot, device) for n, device in enumerate(row_next.get(i, ()) + (sibling,))]

    def col_sends(i):
        slot = col_slot(cols[i])
        base = 16 + sum(len(col_next.get(n, ())) + 1 for n in range(i))
        moves = [copy(base + n, held.at[slot], slot, device) for n, device in enumerate(col_next.get(i, ()))]
        return moves, copy(base + len(moves), held.at[slot], slot, sibling), block_at(q, cols[i]) // 4 != core

    first_slot = col_slot(place_of(p, q))
    flip = copy(15, packed_ref, first_slot, start_place)
    flip.start()

    for move in row_sends(0):
        move.start()
    own = pltpu.make_async_copy(packed_ref, held.at[own_slot], arrive.at[own_slot])
    own.start()

    def row_step(i):
        landed(row_slot(rows[i]))
        if i > 0:
            for move in row_sends(i):
                move.start()

    def col_step(i):
        landed(col_slot(cols[i]))
        moves, across, wanted = col_sends(i)
        for move in moves:
            move.start()

        @pl.when(wanted)
        def _():
            across.start()

    plan = {0: [(row_step, 0)], 2: [(row_step, 1)], 3: [(col_step, 0)], 4: [(row_step, 2), (row_step, 3)],
            6: [(row_step, 4), (row_step, 5)], 8: [(col_step, 1)], 9: [(col_step, 2), (col_step, 3)],
            10: [(row_step, 6)], 12: [(row_step, 7)], 13: [(col_step, 5), (col_step, 4)], 15: [(col_step, 6)],
            20: [(col_step, 7)]}
    near = block_at(q, p) // 4 == core
    wanted_places = [jnp.where(near, cols[a], cols[b]) for a, b in ((0, 1), (2, 4), (3, 5), (6, 7))]
    unit = 2.0 ** -28 / 64.0
    scale = unit / math.sqrt(14336.0)

    def pick(values, i):
        value = values[0]
        for n in range(1, len(values)):
            value = jnp.where(i == n, values[n], value)
        return value

    def half(n):
        low = n_col * EX + 256 * n
        offsets = [pl.multiple_of(lax.rem(block_at(q, m), 4) * 128, 128) for m in wanted_places[2 * n:2 * n + 2]]

        def tile(t, carry):
            at = pl.multiple_of(t * 256, 256)
            total = None
            for k in range(4):
                term = lax.dot_general(
                    panel[pl.ds(at, 256), 2048 * k:2048 * (k + 1)], panel[low:low + 256, 2048 * k:2048 * (k + 1)],
                    (((1,), (1,)), ((), ())), preferred_element_type=F32)
                total = term if total is None else total + term
            for i in range(2):
                out_ref[pl.ds(at, 256), pl.ds(offsets[i], 128)] = total[:, 128 * i:128 * (i + 1)]
            return carry

        lax.fori_loop(0, 4, tile, 0)

    def block(k, carry):
        @pl.when(k == n_col + 4)
        def _():
            half(0)

        for at, steps in plan.items():
            @pl.when(k == at)
            def _():
                for step, i in steps:
                    step(i)

        is_row = k < n_col
        place = jnp.where(is_row, k, k - n_col) // 2
        other = lax.rem(k, 2)
        part = jnp.where(other == 0, core, 1 - core)
        m = jnp.where(is_row, pick(rows, place), pick(wanted_places, place))
        slot = jnp.where(is_row, 0, n_col) + 2 * m + part

        @pl.when(other == 1)
        def _():
            landed(slot)

        row0 = jnp.where(is_row, slot, n_col + 2 * place + part) * EX
        form(held, slot, jnp.where(is_row, scale / 64.0, scale / 128.0), panel, row0,
             g_hi, g_lo, kin, a_work, hi_ref, lo_ref, lhs)
        return carry

    lax.fori_loop(0, n_col + 8, block, 0)
    half(1)

    flip.wait_send()

    for i in range(chips):
        for move in row_sends(i):
            move.wait_send()
        moves, across, wanted = col_sends(i)
        for move in moves:
            move.wait_send()

        @pl.when(wanted)
        def _():
            across.wait_send()


def panels(packed, n_row, n_col):
    per = n_row
    rows, cols = n_col * EX, per * EX
    return pl.pallas_call(
        functools.partial(panel_kernel, n_row, n_col),
        out_shape=pltpu.VMEM((rows, cols), F32),
        in_specs=[pl.BlockSpec(memory_space=pltpu.VMEM)],
        out_specs=pl.BlockSpec(memory_space=pltpu.VMEM),
        scratch_shapes=[
            pltpu.VMEM((2 * n_col, ROWS, LANE), I16),
            pltpu.VMEM((rows + cols, KO * KI), BF16),
            pltpu.VMEM((TOK, KO), BF16),
            pltpu.VMEM((TOK, KO), BF16),
            pltpu.VMEM((4, LANE, LANE), BF16),
            pltpu.VMEM((4, KI + 8, LANE), F32),
            pltpu.VMEM((8, KI, LANE), F32),
            pltpu.VMEM((8, KI, LANE), F32),
            pltpu.VMEM((8, 8 * KI, 2 * LANE), BF16),
            pltpu.SemaphoreType.DMA((32,)),
            pltpu.SemaphoreType.DMA((2 * n_col,)),
        ],
        compiler_params=pltpu.CompilerParams(
            collective_id=0, has_side_effects=True, vmem_limit_bytes=56 << 20),
        cost_estimate=pl.CostEstimate(flops=20 << 30, bytes_accessed=4 << 20, transcendentals=0),
        name="panels",
    )(packed)


def body(n_row, n_col, activations, out_grads, token_counts, proj_seeds):
    packed = project(activations, out_grads, token_counts, proj_seeds)
    return panels(packed, n_row, n_col)


def solution(mesh):
    return jax.shard_map(
        functools.partial(body, mesh.shape["row"], mesh.shape["col"]),
        mesh=mesh,
        in_specs=(P(("row", "col"), None), P(("row", "col"), None), P(("row", "col"), None), P()),
        out_specs=P("row", "col"),
        check_vma=False,
    )
```

```python
import functools
import math

import jax
import jax.numpy as jnp
from jax import lax
from jax.experimental import pallas as pl
from jax.experimental.pallas import tpu as pltpu
from jax.sharding import PartitionSpec as P

KO = 128
KI = 64
MOD = 32749
MESH = pl.DeviceIdType.MESH
F32 = jnp.float32
I32 = jnp.int32
BF16 = jnp.bfloat16
I16 = jnp.int16

TOK = 512
EX = 64
STEPS = 7
AHEAD = 2
ROWS_G = TOK
ROWS_A = ROWS_G + 4 * KI
ROWS = ROWS_A + 16
LANE = 128


def reduced(x):
    q = (x.astype(F32) * (1.0 / MOD)).astype(I32)
    return x - q * MOD


def signs_of(first, second):
    h = reduced(first * first + 5471)
    h = reduced(h * h + second)
    x = h * h + 12007
    q = (x.astype(F32) * (1.0 / MOD) + 0.5).astype(I32)
    r = x - q * MOD
    odd = (r ^ (r >> 31)) & 1
    return jnp.where(odd == 0, 1.0, -1.0).astype(F32).astype(BF16)


def centred(scalar):
    low = scalar - (((scalar >> 7) * 8196) >> 21) * MOD
    return jnp.where(low > MOD // 2, low - MOD, low)


def exponent(largest):
    return jnp.ceil(jnp.log2(jnp.maximum(largest, 1e-30)))


def project_kernel(seeds_ref, counts_ref, act_hbm, grad_hbm, out_ref, act, grad, g_acc, a_acc, s_a, act_sem, grad_sem):
    depth_g = grad.shape[1] // STEPS
    depth_a = act.shape[1] // 8

    def fetch_a(k):
        span = pl.ds(k * (act.shape[1] // 4), act.shape[1] // 4)
        return pltpu.make_async_copy(act_hbm.at[:, span], act.at[:, span], act_sem.at[k])

    def fetch_g(k):
        span = pl.ds(pl.multiple_of(k * depth_g, LANE), depth_g)
        return pltpu.make_async_copy(grad_hbm.at[:, span], grad.at[:, span], grad_sem.at[k])

    for k in range(AHEAD):
        fetch_g(k).start()
    g_acc[...] = jnp.zeros_like(g_acc)
    sub_a = lax.broadcasted_iota(I32, (KI, LANE), 0)
    lane_a = lax.broadcasted_iota(I32, (KI, LANE), 1)

    def part_a(k, carry):
        for part in range(depth_a // LANE):
            start = k * depth_a + part * LANE
            first = (181 * lane_a + 7 * sub_a) + centred(181 * start + seeds_ref[0])
            second = (lane_a + 31 * sub_a) + start
            s_a[:, pl.ds(pl.multiple_of(start, LANE), LANE)] = signs_of(first, second)
        return carry

    places = lax.broadcasted_iota(I32, (1, TOK), 1)

    def tally(e, carry):
        end, owner = carry
        end = end + counts_ref[0, e]
        return end, owner + (places >= end).astype(I32)

    _, owner = lax.fori_loop(0, EX, tally, (jnp.int32(0), jnp.zeros((1, TOK), I32)))
    lax.fori_loop(0, 8, part_a, 0)
    sub = lax.broadcasted_iota(I32, (LANE, KO), 0)
    lane = lax.broadcasted_iota(I32, (LANE, KO), 1)

    def part_g(k, carry):
        fetch_g(k).wait()

        @pl.when(k + AHEAD < STEPS)
        def _():
            fetch_g(k + AHEAD).start()

        for n in range(4):
            @pl.when(k == n + 1)
            def _():
                fetch_a(n).start()

        signs = []
        for part in range(depth_g // LANE):
            start = k * depth_g + part * LANE
            first = (181 * sub + 7 * lane) + centred(181 * start + seeds_ref[1])
            second = (sub + 31 * lane) + start
            signs.append(signs_of(first, second))
        span = pl.ds(pl.multiple_of(k * depth_g, LANE), depth_g)
        g_acc[...] += jnp.dot(grad[:, span], jnp.concatenate(signs, axis=0), preferred_element_type=F32)
        return carry

    lax.fori_loop(0, STEPS, part_g, 0)
    for k in range(4):
        fetch_a(k).wait()
    a_acc[...] = lax.dot_general(
        s_a[...], act[...], (((1,), (1,)), ((), ())), preferred_element_type=F32
    )
    g = g_acc[...]
    a = a_acc[...]
    size = jnp.abs(g)
    g_up = exponent(jnp.max(size, axis=1, keepdims=True))
    g_across = exponent(jnp.max(size.T, axis=0, keepdims=True))
    a_up = exponent(jnp.max(jnp.abs(a), axis=0, keepdims=True))
    out_ref[0:ROWS_G, :] = jnp.round(g * jnp.exp2(14.0 - g_up)).astype(I32).astype(I16)
    a = jnp.round(a * jnp.exp2(14.0 - a_up)).astype(I32).astype(I16)
    total = g_across + a_up
    facts = [total.astype(I32)[:, LANE * k:LANE * (k + 1)] for k in range(4)]
    facts += [owner[:, LANE * k:LANE * (k + 1)] for k in range(4)]
    out_ref[ROWS_A:, :] = jnp.concatenate(facts + [jnp.zeros((8, LANE), I32)], axis=0).astype(I16)
    for k in range(4):
        out_ref[ROWS_G + KI * k:ROWS_G + KI * (k + 1), :] = a[:, LANE * k:LANE * (k + 1)]


def project(activations, out_grads, counts, seeds):
    depth_a = activations.shape[1]
    depth_g = out_grads.shape[1]
    return pl.pallas_call(
        project_kernel,
        out_shape=jax.ShapeDtypeStruct((ROWS, LANE), I16),
        in_specs=[
            pl.BlockSpec(memory_space=pltpu.SMEM),
            pl.BlockSpec(memory_space=pltpu.SMEM),
            pl.BlockSpec(memory_space=pl.ANY),
            pl.BlockSpec(memory_space=pl.ANY),
        ],
        out_specs=pl.BlockSpec(memory_space=pltpu.VMEM),
        scratch_shapes=[
            pltpu.VMEM((TOK, depth_a), BF16),
            pltpu.VMEM((TOK, depth_g), BF16),
            pltpu.VMEM((TOK, KO), F32),
            pltpu.VMEM((KI, TOK), F32),
            pltpu.VMEM((KI, depth_a), BF16),
            pltpu.SemaphoreType.DMA((4,)),
            pltpu.SemaphoreType.DMA((STEPS,)),
        ],
        compiler_params=pltpu.CompilerParams(vmem_limit_bytes=60 << 20),
        cost_estimate=pl.CostEstimate(flops=4 << 30, bytes_accessed=19 << 20, transcendentals=0),
        name="project",
    )(seeds, counts, activations, out_grads)


def form(held, slot, scale, target, row0, g_hi, g_lo, kin, a_work, hi_ref, lo_ref, lhs):
    g = held[slot, 0:ROWS_G, :].astype(I32).astype(F32)
    high = g.astype(BF16)
    g_hi[...] = high
    g_lo[...] = (g - high.astype(F32)).astype(BF16)
    facts = held[slot, ROWS_A:, :].astype(I32)
    for k in range(4):
        sizes = jnp.exp2(facts[k:k + 1, :].astype(F32)) * scale
        owner = facts[4 + k:5 + k, :]
        part = held[slot, ROWS_G + KI * k:ROWS_G + KI * (k + 1), :].astype(I32).astype(F32)
        a_work[k, 0:KI, :] = part * sizes
        a_work[k, KI:KI + 8, :] = jnp.broadcast_to(owner.astype(F32), (8, LANE))
        kin[k] = jnp.broadcast_to((owner >> 3).astype(F32), (LANE, LANE)).T.astype(BF16)
    sub = lax.broadcasted_iota(I32, (16, LANE), 0) & 7
    halves = []
    for group in range(8):
        low = 8 * group
        near = max(low, LANE * (group - 4)) // LANE
        far = (min(LANE * (group + 1), TOK - 8 * (7 - group)) - 1) // LANE
        a = a_work[near].reshape(KI // 8 + 1, 8, LANE)
        above, below = g_hi[LANE * near:LANE * (near + 1), :], g_lo[LANE * near:LANE * (near + 1), :]
        for k in range(near + 1, far + 1):
            owner = a_work[k, KI:KI + 8, :]
            mine = ((owner >= float(low)) & (owner < float(low + 8)))[None]
            a = jnp.where(mine, a_work[k].reshape(KI // 8 + 1, 8, LANE), a)
            mine = kin[k] == jnp.bfloat16(group)
            above = jnp.where(mine, g_hi[LANE * k:LANE * (k + 1), :], above)
            below = jnp.where(mine, g_lo[LANE * k:LANE * (k + 1), :], below)
        owner = jnp.concatenate([a[KI // 8]] * 2, axis=0)
        member = jnp.where(owner == (sub + low).astype(F32), 1.0, 0.0).astype(BF16)
        a = a[:KI // 8].reshape(KI, LANE)
        hi = a.astype(BF16).astype(F32)
        hi_ref[group] = hi
        lo_ref[group] = a - hi
        for j in range(0, KI, 2):
            for k, ref in enumerate((hi_ref, lo_ref)):
                rows = [jnp.broadcast_to(ref[group, j + n:j + n + 1, :], (8, LANE)) for n in range(2)]
                tile = jnp.concatenate(rows, axis=0).astype(BF16) * member
                lhs[group, 8 * j:8 * j + 16, LANE * k:LANE * (k + 1)] = tile
        weights = jnp.concatenate([above, below], axis=1)
        weights = jnp.concatenate([weights, weights], axis=0)
        both = jnp.dot(lhs[group], weights, preferred_element_type=F32)
        halves.append((both[:, :LANE] + both[:, LANE:]).reshape(KI, 8, LANE))
        if group % 2 == 1:
            features = jnp.concatenate(halves, axis=1).astype(BF16)
            halves = []
            at = pl.multiple_of(row0 + (group // 2) * 16, 16)
            for j in range(KI):
                target[pl.ds(at, 16), LANE * j:LANE * (j + 1)] = features[j]


def panel_kernel(n_row, n_col, packed_ref, out_ref, held, panel, g_hi, g_lo, kin, a_work, hi_ref, lo_ref, lhs,
                 send, arrive):
    p = lax.axis_index("row")
    core = lax.rem(lax.axis_index("col"), 2)
    q = lax.axis_index("col") // 2
    chips = n_col // 2

    def pair_q(m):
        return lax.rem(m + 4, 8)

    def ring_q(m, k):
        return (m // 4) * 4 + lax.rem(m + k, 4)

    def pair_p(m):
        return m + 1 - 2 * lax.rem(m, 2)

    def ring_p(m, k):
        return lax.rem(m + 2 * k, 8)

    sibling = (p, 2 * q + 1 - core)

    def place_of(panel, j):
        high = lax.rem(panel + j // 4 + panel // 4, 2)
        return 2 * lax.rem(panel // 2 + 2 + panel - j + 8, 4) + high

    def block_at(panel, m):
        x_lo = lax.rem(panel // 4 + panel + m, 2)
        return 4 * x_lo + lax.rem(panel + 2 + panel // 2 - m // 2 + 8, 4)

    start_place = (place_of(p, q), 2 * p + core)
    start_source = (q, 2 * block_at(q, p) + core)
    row_pair, row_up, row_down = [(p, 2 * m + core) for m in (pair_q(q), ring_q(q, 1), ring_q(q, 3))]
    col_pair, col_up, col_down = [(m, 2 * q + core) for m in (pair_p(p), ring_p(p, 1), ring_p(p, 3))]

    barrier = pltpu.get_barrier_semaphore()
    for other in (sibling, row_pair, row_up, row_down, col_pair, col_up, col_down):
        pl.semaphore_signal(barrier, inc=1, device_id=other, device_id_type=MESH)

    pl.semaphore_signal(barrier, inc=1, device_id=start_source, device_id_type=MESH)
    pl.semaphore_wait(barrier, 8)

    def row_slot(m):
        return 2 * m + core

    def col_slot(m):
        return n_col + 2 * m + core

    def copy(number, source, slot, device):
        return pltpu.make_async_remote_copy(
            src_ref=source, dst_ref=held.at[slot], send_sem=send.at[number], recv_sem=arrive.at[slot],
            device_id=device, device_id_type=MESH)

    def landed(slot):
        copy(0, held.at[slot], slot, sibling).wait_recv()

    own_slot = row_slot(q)
    rows = [q, pair_q(q), ring_q(q, 3), ring_q(q, 1), pair_q(ring_q(q, 3)), pair_q(ring_q(q, 1)), ring_q(q, 2),
            pair_q(ring_q(q, 2))]
    cols = [p, pair_p(p), ring_p(p, 3), ring_p(p, 1), pair_p(ring_p(p, 3)), pair_p(ring_p(p, 1)), ring_p(p, 2),
            pair_p(ring_p(p, 2))]
    row_next = {0: (row_pair, row_up, row_down), 1: (row_up, row_down), 2: (row_up,), 5: (row_down,)}
    col_next = {0: (col_pair, col_up, col_down), 1: (col_up, col_down), 2: (col_up,), 5: (col_down,)}

    def row_sends(i):
        slot = row_slot(rows[i])
        source = packed_ref if i == 0 else held.at[slot]
        base = 0 if i == 0 else sum(len(row_next.get(n, ())) + 1 for n in range(i))
        return [copy(base + n, source, slot, device) for n, device in enumerate(row_next.get(i, ()) + (sibling,))]

    def col_sends(i):
        slot = col_slot(cols[i])
        base = 16 + sum(len(col_next.get(n, ())) + 1 for n in range(i))
        moves = [copy(base + n, held.at[slot], slot, device) for n, device in enumerate(col_next.get(i, ()))]
        return moves, copy(base + len(moves), held.at[slot], slot, sibling), block_at(q, cols[i]) // 4 != core

    first_slot = col_slot(place_of(p, q))
    flip = copy(15, packed_ref, first_slot, start_place)
    flip.start()

    for move in row_sends(0):
        move.start()
    own = pltpu.make_async_copy(packed_ref, held.at[own_slot], arrive.at[own_slot])
    own.start()

    def row_step(i):
        landed(row_slot(rows[i]))
        if i > 0:
            for move in row_sends(i):
                move.start()

    def col_step(i):
        landed(col_slot(cols[i]))
        moves, across, wanted = col_sends(i)
        for move in moves:
            move.start()

        @pl.when(wanted)
        def _():
            across.start()

    plan = {0: [(row_step, 0)], 2: [(row_step, 1)], 3: [(col_step, 0)], 4: [(row_step, 2), (row_step, 3)],
            6: [(row_step, 4), (row_step, 5)], 8: [(col_step, 1)], 9: [(col_step, 2), (col_step, 3)],
            10: [(row_step, 6)], 12: [(row_step, 7)], 13: [(col_step, 5), (col_step, 4)], 15: [(col_step, 6)],
            20: [(col_step, 7)]}
    near = block_at(q, p) // 4 == core
    wanted_places = [jnp.where(near, cols[a], cols[b]) for a, b in ((0, 1), (2, 4), (3, 5), (6, 7))]
    unit = 2.0 ** -28 / 64.0
    scale = unit / math.sqrt(14336.0)

    def pick(values, i):
        value = values[0]
        for n in range(1, len(values)):
            value = jnp.where(i == n, values[n], value)
        return value

    def half(n):
        low = n_col * EX + 256 * n
        offsets = [pl.multiple_of(lax.rem(block_at(q, m), 4) * 128, 128) for m in wanted_places[2 * n:2 * n + 2]]

        def tile(t, carry):
            at = pl.multiple_of(t * 256, 256)
            total = None
            for k in range(4):
                term = lax.dot_general(
                    panel[pl.ds(at, 256), 2048 * k:2048 * (k + 1)], panel[low:low + 256, 2048 * k:2048 * (k + 1)],
                    (((1,), (1,)), ((), ())), preferred_element_type=F32)
                total = term if total is None else total + term
            for i in range(2):
                out_ref[pl.ds(at, 256), pl.ds(offsets[i], 128)] = total[:, 128 * i:128 * (i + 1)]
            return carry

        lax.fori_loop(0, 4, tile, 0)

    def block(k, carry):
        @pl.when(k == n_col + 4)
        def _():
            half(0)

        for at, steps in plan.items():
            @pl.when(k == at)
            def _():
                for step, i in steps:
                    step(i)

        is_row = k < n_col
        place = jnp.where(is_row, k, k - n_col) // 2
        other = lax.rem(k, 2)
        part = jnp.where(other == 0, core, 1 - core)
        m = jnp.where(is_row, pick(rows, place), pick(wanted_places, place))
        slot = jnp.where(is_row, 0, n_col) + 2 * m + part

        @pl.when(other == 1)
        def _():
            landed(slot)

        row0 = jnp.where(is_row, slot, n_col + 2 * place + part) * EX
        form(held, slot, jnp.where(is_row, scale / 64.0, scale / 128.0), panel, row0,
             g_hi, g_lo, kin, a_work, hi_ref, lo_ref, lhs)
        return carry

    lax.fori_loop(0, n_col + 8, block, 0)
    half(1)

    flip.wait_send()

    for i in range(chips):
        for move in row_sends(i):
            move.wait_send()
        moves, across, wanted = col_sends(i)
        for move in moves:
            move.wait_send()

        @pl.when(wanted)
        def _():
            across.wait_send()


def panels(packed, n_row, n_col):
    per = n_row
    rows, cols = n_col * EX, per * EX
    return pl.pallas_call(
        functools.partial(panel_kernel, n_row, n_col),
        out_shape=pltpu.VMEM((rows, cols), F32),
        in_specs=[pl.BlockSpec(memory_space=pl.ANY)],
        out_specs=pl.BlockSpec(memory_space=pltpu.VMEM),
        scratch_shapes=[
            pltpu.VMEM((2 * n_col, ROWS, LANE), I16),
            pltpu.VMEM((rows + cols, KO * KI), BF16),
            pltpu.VMEM((TOK, KO), BF16),
            pltpu.VMEM((TOK, KO), BF16),
            pltpu.VMEM((4, LANE, LANE), BF16),
            pltpu.VMEM((4, KI + 8, LANE), F32),
            pltpu.VMEM((8, KI, LANE), F32),
            pltpu.VMEM((8, KI, LANE), F32),
            pltpu.VMEM((8, 8 * KI, 2 * LANE), BF16),
            pltpu.SemaphoreType.DMA((32,)),
            pltpu.SemaphoreType.DMA((2 * n_col,)),
        ],
        compiler_params=pltpu.CompilerParams(
            collective_id=0, has_side_effects=True, vmem_limit_bytes=56 << 20),
        cost_estimate=pl.CostEstimate(flops=20 << 30, bytes_accessed=4 << 20, transcendentals=0),
        name="panels",
    )(packed)


def body(n_row, n_col, activations, out_grads, token_counts, proj_seeds):
    packed = project(activations, out_grads, token_counts, proj_seeds)
    return panels(packed, n_row, n_col)


def solution(mesh):
    return jax.shard_map(
        functools.partial(body, mesh.shape["row"], mesh.shape["col"]),
        mesh=mesh,
        in_specs=(P(("row", "col"), None), P(("row", "col"), None), P(("row", "col"), None), P()),
        out_specs=P("row", "col"),
        check_vma=False,
    )
```

```python
import functools
import math

import jax
import jax.numpy as jnp
from jax import lax
from jax.experimental import pallas as pl
from jax.experimental.pallas import tpu as pltpu
from jax.sharding import PartitionSpec as P

KO = 128
KI = 64
MOD = 32749
MESH = pl.DeviceIdType.MESH
F32 = jnp.float32
I32 = jnp.int32
BF16 = jnp.bfloat16
I16 = jnp.int16

TOK = 512
EX = 64
STEPS = 7
AHEAD = 2
ROWS_G = TOK
ROWS_A = ROWS_G + 4 * KI
ROWS = ROWS_A + 16
LANE = 128


def reduced(x):
    q = (x.astype(F32) * (1.0 / MOD)).astype(I32)
    return x - q * MOD


def signs_of(first, second):
    h = reduced(first * first + 5471)
    h = reduced(h * h + second)
    x = h * h + 12007
    q = (x.astype(F32) * (1.0 / MOD) + 0.5).astype(I32)
    r = x - q * MOD
    odd = (r ^ (r >> 31)) & 1
    return jnp.where(odd == 0, 1.0, -1.0).astype(F32).astype(BF16)


def centred(scalar):
    low = scalar - (((scalar >> 7) * 8196) >> 21) * MOD
    return jnp.where(low > MOD // 2, low - MOD, low)


def exponent(largest):
    return jnp.ceil(jnp.log2(jnp.maximum(largest, 1e-30)))


def project_kernel(seeds_ref, counts_ref, act_hbm, grad_hbm, out_ref, act, grad, g_acc, a_acc, s_a, act_sem, grad_sem):
    depth_g = grad.shape[1] // STEPS
    depth_a = act.shape[1] // 8

    def fetch_a(k):
        span = pl.ds(k * (act.shape[1] // 4), act.shape[1] // 4)
        return pltpu.make_async_copy(act_hbm.at[:, span], act.at[:, span], act_sem.at[k])

    def fetch_g(k):
        span = pl.ds(pl.multiple_of(k * depth_g, LANE), depth_g)
        return pltpu.make_async_copy(grad_hbm.at[:, span], grad.at[:, span], grad_sem.at[k])

    for k in range(AHEAD):
        fetch_g(k).start()
    g_acc[...] = jnp.zeros_like(g_acc)
    sub_a = lax.broadcasted_iota(I32, (KI, LANE), 0)
    lane_a = lax.broadcasted_iota(I32, (KI, LANE), 1)

    def part_a(k, carry):
        for part in range(depth_a // LANE):
            start = k * depth_a + part * LANE
            first = (181 * lane_a + 7 * sub_a) + centred(181 * start + seeds_ref[0])
            second = (lane_a + 31 * sub_a) + start
            s_a[:, pl.ds(pl.multiple_of(start, LANE), LANE)] = signs_of(first, second)
        return carry

    places = lax.broadcasted_iota(I32, (1, TOK), 1)

    def tally(e, carry):
        end, owner = carry
        end = end + counts_ref[0, e]
        return end, owner + (places >= end).astype(I32)

    _, owner = lax.fori_loop(0, EX, tally, (jnp.int32(0), jnp.zeros((1, TOK), I32)))
    lax.fori_loop(0, 8, part_a, 0)
    sub = lax.broadcasted_iota(I32, (LANE, KO), 0)
    lane = lax.broadcasted_iota(I32, (LANE, KO), 1)

    def part_g(k, carry):
        fetch_g(k).wait()

        @pl.when(k + AHEAD < STEPS)
        def _():
            fetch_g(k + AHEAD).start()

        for n in range(4):
            @pl.when(k == n + 1)
            def _():
                fetch_a(n).start()

        signs = []
        for part in range(depth_g // LANE):
            start = k * depth_g + part * LANE
            first = (181 * sub + 7 * lane) + centred(181 * start + seeds_ref[1])
            second = (sub + 31 * lane) + start
            signs.append(signs_of(first, second))
        span = pl.ds(pl.multiple_of(k * depth_g, LANE), depth_g)
        g_acc[...] += jnp.dot(grad[:, span], jnp.concatenate(signs, axis=0), preferred_element_type=F32)
        return carry

    lax.fori_loop(0, STEPS, part_g, 0)
    for k in range(4):
        fetch_a(k).wait()
    a_acc[...] = lax.dot_general(
        s_a[...], act[...], (((1,), (1,)), ((), ())), preferred_element_type=F32
    )
    g = g_acc[...]
    a = a_acc[...]
    size = jnp.abs(g)
    g_up = exponent(jnp.max(size, axis=1, keepdims=True))
    g_across = exponent(jnp.max(size.T, axis=0, keepdims=True))
    a_up = exponent(jnp.max(jnp.abs(a), axis=0, keepdims=True))
    out_ref[0:ROWS_G, :] = jnp.round(g * jnp.exp2(14.0 - g_up)).astype(I32).astype(I16)
    a = jnp.round(a * jnp.exp2(14.0 - a_up)).astype(I32).astype(I16)
    total = g_across + a_up
    facts = [total.astype(I32)[:, LANE * k:LANE * (k + 1)] for k in range(4)]
    facts += [owner[:, LANE * k:LANE * (k + 1)] for k in range(4)]
    out_ref[ROWS_A:, :] = jnp.concatenate(facts + [jnp.zeros((8, LANE), I32)], axis=0).astype(I16)
    for k in range(4):
        out_ref[ROWS_G + KI * k:ROWS_G + KI * (k + 1), :] = a[:, LANE * k:LANE * (k + 1)]


def project(activations, out_grads, counts, seeds):
    depth_a = activations.shape[1]
    depth_g = out_grads.shape[1]
    return pl.pallas_call(
        project_kernel,
        out_shape=jax.ShapeDtypeStruct((ROWS, LANE), I16),
        in_specs=[
            pl.BlockSpec(memory_space=pltpu.SMEM),
            pl.BlockSpec(memory_space=pltpu.SMEM),
            pl.BlockSpec(memory_space=pl.ANY),
            pl.BlockSpec(memory_space=pl.ANY),
        ],
        out_specs=pl.BlockSpec(memory_space=pltpu.VMEM),
        scratch_shapes=[
            pltpu.VMEM((TOK, depth_a), BF16),
            pltpu.VMEM((TOK, depth_g), BF16),
            pltpu.VMEM((TOK, KO), F32),
            pltpu.VMEM((KI, TOK), F32),
            pltpu.VMEM((KI, depth_a), BF16),
            pltpu.SemaphoreType.DMA((4,)),
            pltpu.SemaphoreType.DMA((STEPS,)),
        ],
        compiler_params=pltpu.CompilerParams(vmem_limit_bytes=60 << 20),
        cost_estimate=pl.CostEstimate(flops=4 << 30, bytes_accessed=19 << 20, transcendentals=0),
        name="project",
    )(seeds, counts, activations, out_grads)


def form(held, slot, scale, target, row0, g_hi, g_lo, kin, a_work, hi_ref, lo_ref, lhs):
    g = held[slot, 0:ROWS_G, :].astype(I32).astype(F32)
    high = g.astype(BF16)
    g_hi[...] = high
    g_lo[...] = (g - high.astype(F32)).astype(BF16)
    facts = held[slot, ROWS_A:, :].astype(I32)
    for k in range(4):
        sizes = jnp.exp2(facts[k:k + 1, :].astype(F32)) * scale
        owner = facts[4 + k:5 + k, :]
        part = held[slot, ROWS_G + KI * k:ROWS_G + KI * (k + 1), :].astype(I32).astype(F32)
        a_work[k, 0:KI, :] = part * sizes
        a_work[k, KI:KI + 8, :] = jnp.broadcast_to(owner.astype(F32), (8, LANE))
        kin[k] = jnp.broadcast_to((owner >> 3).astype(F32), (LANE, LANE)).T.astype(BF16)
    sub = lax.broadcasted_iota(I32, (16, LANE), 0) & 7
    halves = []
    for group in range(8):
        low = 8 * group
        near = max(low, LANE * (group - 4)) // LANE
        far = (min(LANE * (group + 1), TOK - 8 * (7 - group)) - 1) // LANE
        a = a_work[near].reshape(KI // 8 + 1, 8, LANE)
        above, below = g_hi[LANE * near:LANE * (near + 1), :], g_lo[LANE * near:LANE * (near + 1), :]
        for k in range(near + 1, far + 1):
            owner = a_work[k, KI:KI + 8, :]
            mine = ((owner >= float(low)) & (owner < float(low + 8)))[None]
            a = jnp.where(mine, a_work[k].reshape(KI // 8 + 1, 8, LANE), a)
            mine = kin[k] == jnp.bfloat16(group)
            above = jnp.where(mine, g_hi[LANE * k:LANE * (k + 1), :], above)
            below = jnp.where(mine, g_lo[LANE * k:LANE * (k + 1), :], below)
        owner = jnp.concatenate([a[KI // 8]] * 2, axis=0)
        member = jnp.where(owner == (sub + low).astype(F32), 1.0, 0.0).astype(BF16)
        a = a[:KI // 8].reshape(KI, LANE)
        hi = a.astype(BF16).astype(F32)
        hi_ref[group] = hi
        lo_ref[group] = a - hi
        for j in range(0, KI, 2):
            for k, ref in enumerate((hi_ref, lo_ref)):
                rows = [jnp.broadcast_to(ref[group, j + n:j + n + 1, :], (8, LANE)) for n in range(2)]
                tile = jnp.concatenate(rows, axis=0).astype(BF16) * member
                lhs[group, 8 * j:8 * j + 16, LANE * k:LANE * (k + 1)] = tile
        weights = jnp.concatenate([above, below], axis=1)
        weights = jnp.concatenate([weights, weights], axis=0)
        both = jnp.dot(lhs[group], weights, preferred_element_type=F32)
        halves.append((both[:, :LANE] + both[:, LANE:]).reshape(KI, 8, LANE))
        if group % 2 == 1:
            features = jnp.concatenate(halves, axis=1).astype(BF16)
            halves = []
            at = pl.multiple_of(row0 + (group // 2) * 16, 16)
            for j in range(KI):
                target[pl.ds(at, 16), LANE * j:LANE * (j + 1)] = features[j]


def panel_kernel(n_row, n_col, packed_ref, out_ref, held, panel, g_hi, g_lo, kin, a_work, hi_ref, lo_ref, lhs,
                 send, arrive):
    p = lax.axis_index("row")
    core = lax.rem(lax.axis_index("col"), 2)
    q = lax.axis_index("col") // 2
    chips = n_col // 2

    def pair_q(m):
        return lax.rem(m + 4, 8)

    def ring_q(m, k):
        return (m // 4) * 4 + lax.rem(m + k, 4)

    def pair_p(m):
        return m + 1 - 2 * lax.rem(m, 2)

    def ring_p(m, k):
        return lax.rem(m + 2 * k, 8)

    sibling = (p, 2 * q + 1 - core)

    def place_of(panel, j):
        high = lax.rem(panel + j // 4 + panel // 4, 2)
        return 2 * lax.rem(panel // 2 + 2 + panel - j + 8, 4) + high

    def block_at(panel, m):
        x_lo = lax.rem(panel // 4 + panel + m, 2)
        return 4 * x_lo + lax.rem(panel + 2 + panel // 2 - m // 2 + 8, 4)

    start_place = (place_of(p, q), 2 * p + core)
    start_source = (q, 2 * block_at(q, p) + core)
    row_pair, row_up, row_down = [(p, 2 * m + core) for m in (pair_q(q), ring_q(q, 1), ring_q(q, 3))]
    col_pair, col_up, col_down = [(m, 2 * q + core) for m in (pair_p(p), ring_p(p, 1), ring_p(p, 3))]

    barrier = pltpu.get_barrier_semaphore()
    for other in (sibling, row_pair, row_up, row_down, col_pair, col_up, col_down):
        pl.semaphore_signal(barrier, inc=1, device_id=other, device_id_type=MESH)

    pl.semaphore_signal(barrier, inc=1, device_id=start_source, device_id_type=MESH)
    pl.semaphore_wait(barrier, 8)

    def row_slot(m):
        return 2 * m + core

    def col_slot(m):
        return n_col + 2 * m + core

    def copy(number, source, slot, device):
        return pltpu.make_async_remote_copy(
            src_ref=source, dst_ref=held.at[slot], send_sem=send.at[number], recv_sem=arrive.at[slot],
            device_id=device, device_id_type=MESH)

    def landed(slot):
        copy(0, held.at[slot], slot, sibling).wait_recv()

    own_slot = row_slot(q)
    rows = [q, pair_q(q), ring_q(q, 3), ring_q(q, 1), pair_q(ring_q(q, 3)), pair_q(ring_q(q, 1)), ring_q(q, 2),
            pair_q(ring_q(q, 2))]
    cols = [p, pair_p(p), ring_p(p, 3), ring_p(p, 1), pair_p(ring_p(p, 3)), pair_p(ring_p(p, 1)), ring_p(p, 2),
            pair_p(ring_p(p, 2))]
    row_next = {0: (row_pair, row_up, row_down), 1: (row_up, row_down), 2: (row_up,), 5: (row_down,)}
    col_next = {0: (col_pair, col_up, col_down), 1: (col_up, col_down), 2: (col_up,), 5: (col_down,)}

    def row_sends(i):
        slot = row_slot(rows[i])
        source = packed_ref if i == 0 else held.at[slot]
        base = 0 if i == 0 else sum(len(row_next.get(n, ())) + 1 for n in range(i))
        return [copy(base + n, source, slot, device) for n, device in enumerate((sibling,) + row_next.get(i, ()))]

    def col_sends(i):
        slot = col_slot(cols[i])
        base = 16 + sum(len(col_next.get(n, ())) + 1 for n in range(i))
        moves = [copy(base + n, held.at[slot], slot, device) for n, device in enumerate(col_next.get(i, ()))]
        return moves, copy(base + len(moves), held.at[slot], slot, sibling), block_at(q, cols[i]) // 4 != core

    first_slot = col_slot(place_of(p, q))
    flip = copy(15, packed_ref, first_slot, start_place)
    own = pltpu.make_async_copy(packed_ref, held.at[own_slot], arrive.at[own_slot])
    own.start()
    to_sibling, *to_others = row_sends(0)
    to_sibling.start()
    flip.start()
    for move in to_others:
        move.start()

    def row_step(i):
        landed(row_slot(rows[i]))
        if i > 0:
            for move in row_sends(i):
                move.start()

    def col_step(i):
        landed(col_slot(cols[i]))
        moves, across, wanted = col_sends(i)

        @pl.when(wanted)
        def _():
            across.start()

        for move in moves:
            move.start()

    plan = {0: [(row_step, 0)], 2: [(row_step, 1)], 3: [(col_step, 0)], 4: [(row_step, 2), (row_step, 3)],
            6: [(row_step, 4), (row_step, 5)], 8: [(col_step, 1)], 9: [(col_step, 2), (col_step, 3)],
            10: [(row_step, 6)], 12: [(row_step, 7)], 13: [(col_step, 5), (col_step, 4)], 15: [(col_step, 6)],
            20: [(col_step, 7)]}
    near = block_at(q, p) // 4 == core
    wanted_places = [jnp.where(near, cols[a], cols[b]) for a, b in ((0, 1), (2, 4), (3, 5), (6, 7))]
    unit = 2.0 ** -28 / 64.0
    scale = unit / math.sqrt(14336.0)

    def pick(values, i):
        value = values[0]
        for n in range(1, len(values)):
            value = jnp.where(i == n, values[n], value)
        return value

    def half(n):
        low = n_col * EX + 256 * n
        offsets = [pl.multiple_of(lax.rem(block_at(q, m), 4) * 128, 128) for m in wanted_places[2 * n:2 * n + 2]]

        def tile(t, carry):
            at = pl.multiple_of(t * 256, 256)
            total = None
            for k in range(4):
                term = lax.dot_general(
                    panel[pl.ds(at, 256), 2048 * k:2048 * (k + 1)], panel[low:low + 256, 2048 * k:2048 * (k + 1)],
                    (((1,), (1,)), ((), ())), preferred_element_type=F32)
                total = term if total is None else total + term
            for i in range(2):
                out_ref[pl.ds(at, 256), pl.ds(offsets[i], 128)] = total[:, 128 * i:128 * (i + 1)]
            return carry

        lax.fori_loop(0, 4, tile, 0)

    def block(k, carry):
        @pl.when(k == n_col + 4)
        def _():
            half(0)

        for at, steps in plan.items():
            @pl.when(k == at)
            def _():
                for step, i in steps:
                    step(i)

        is_row = k < n_col
        place = jnp.where(is_row, k, k - n_col) // 2
        other = lax.rem(k, 2)
        part = jnp.where(other == 0, core, 1 - core)
        m = jnp.where(is_row, pick(rows, place), pick(wanted_places, place))
        slot = jnp.where(is_row, 0, n_col) + 2 * m + part

        @pl.when(other == 1)
        def _():
            landed(slot)

        row0 = jnp.where(is_row, slot, n_col + 2 * place + part) * EX
        form(held, slot, jnp.where(is_row, scale / 64.0, scale / 128.0), panel, row0,
             g_hi, g_lo, kin, a_work, hi_ref, lo_ref, lhs)
        return carry

    lax.fori_loop(0, n_col + 8, block, 0)
    half(1)

    flip.wait_send()

    for i in range(chips):
        for move in row_sends(i):
            move.wait_send()
        moves, across, wanted = col_sends(i)
        for move in moves:
            move.wait_send()

        @pl.when(wanted)
        def _():
            across.wait_send()


def panels(packed, n_row, n_col):
    per = n_row
    rows, cols = n_col * EX, per * EX
    return pl.pallas_call(
        functools.partial(panel_kernel, n_row, n_col),
        out_shape=pltpu.VMEM((rows, cols), F32),
        in_specs=[pl.BlockSpec(memory_space=pl.ANY)],
        out_specs=pl.BlockSpec(memory_space=pltpu.VMEM),
        scratch_shapes=[
            pltpu.VMEM((2 * n_col, ROWS, LANE), I16),
            pltpu.VMEM((rows + cols, KO * KI), BF16),
            pltpu.VMEM((TOK, KO), BF16),
            pltpu.VMEM((TOK, KO), BF16),
            pltpu.VMEM((4, LANE, LANE), BF16),
            pltpu.VMEM((4, KI + 8, LANE), F32),
            pltpu.VMEM((8, KI, LANE), F32),
            pltpu.VMEM((8, KI, LANE), F32),
            pltpu.VMEM((8, 8 * KI, 2 * LANE), BF16),
            pltpu.SemaphoreType.DMA((32,)),
            pltpu.SemaphoreType.DMA((2 * n_col,)),
        ],
        compiler_params=pltpu.CompilerParams(
            collective_id=0, has_side_effects=True, vmem_limit_bytes=56 << 20),
        cost_estimate=pl.CostEstimate(flops=20 << 30, bytes_accessed=4 << 20, transcendentals=0),
        name="panels",
    )(packed)


def body(n_row, n_col, activations, out_grads, token_counts, proj_seeds):
    packed = project(activations, out_grads, token_counts, proj_seeds)
    return panels(packed, n_row, n_col)


def solution(mesh):
    return jax.shard_map(
        functools.partial(body, mesh.shape["row"], mesh.shape["col"]),
        mesh=mesh,
        in_specs=(P(("row", "col"), None), P(("row", "col"), None), P(("row", "col"), None), P()),
        out_specs=P("row", "col"),
        check_vma=False,
    )
```

```python
import functools
import math

import jax
import jax.numpy as jnp
from jax import lax
from jax.experimental import pallas as pl
from jax.experimental.pallas import tpu as pltpu
from jax.sharding import PartitionSpec as P

KO = 128
KI = 64
MOD = 32749
MESH = pl.DeviceIdType.MESH
F32 = jnp.float32
I32 = jnp.int32
BF16 = jnp.bfloat16
I16 = jnp.int16

TOK = 512
EX = 64
STEPS = 4
AHEAD = 1
ROWS_G = TOK
ROWS_A = ROWS_G + 4 * KI
ROWS = ROWS_A + 16
LANE = 128


def reduced(x):
    q = (x.astype(F32) * (1.0 / MOD)).astype(I32)
    return x - q * MOD


def signs_of(first, second):
    h = reduced(first * first + 5471)
    h = reduced(h * h + second)
    x = h * h + 12007
    q = (x.astype(F32) * (1.0 / MOD) + 0.5).astype(I32)
    r = x - q * MOD
    odd = (r ^ (r >> 31)) & 1
    return jnp.where(odd == 0, 1.0, -1.0).astype(F32).astype(BF16)


def centred(scalar):
    low = scalar - (((scalar >> 7) * 8196) >> 21) * MOD
    return jnp.where(low > MOD // 2, low - MOD, low)


def exponent(largest):
    return jnp.ceil(jnp.log2(jnp.maximum(largest, 1e-30)))


def project_kernel(seeds_ref, counts_ref, act_hbm, grad_hbm, out_ref, act, grad, g_acc, a_acc, s_a, act_sem, grad_sem):
    depth_g = grad.shape[1] // STEPS
    depth_a = act.shape[1] // 8

    def fetch_a(k):
        span = pl.ds(k * (act.shape[1] // 4), act.shape[1] // 4)
        return pltpu.make_async_copy(act_hbm.at[:, span], act.at[:, span], act_sem.at[k])

    def fetch_g(k):
        span = pl.ds(pl.multiple_of(k * depth_g, LANE), depth_g)
        return pltpu.make_async_copy(grad_hbm.at[:, span], grad.at[:, span], grad_sem.at[k])

    for k in range(AHEAD):
        fetch_g(k).start()
    g_acc[...] = jnp.zeros_like(g_acc)
    sub_a = lax.broadcasted_iota(I32, (KI, LANE), 0)
    lane_a = lax.broadcasted_iota(I32, (KI, LANE), 1)

    def part_a(k, carry):
        for part in range(depth_a // LANE):
            start = k * depth_a + part * LANE
            first = (181 * lane_a + 7 * sub_a) + centred(181 * start + seeds_ref[0])
            second = (lane_a + 31 * sub_a) + start
            s_a[:, pl.ds(pl.multiple_of(start, LANE), LANE)] = signs_of(first, second)
        return carry

    places = lax.broadcasted_iota(I32, (1, TOK), 1)

    def tally(e, carry):
        end, owner = carry
        end = end + counts_ref[0, e]
        return end, owner + (places >= end).astype(I32)

    _, owner = lax.fori_loop(0, EX, tally, (jnp.int32(0), jnp.zeros((1, TOK), I32)))
    lax.fori_loop(0, 8, part_a, 0)
    sub = lax.broadcasted_iota(I32, (LANE, KO), 0)
    lane = lax.broadcasted_iota(I32, (LANE, KO), 1)

    def part_g(k, carry):
        fetch_g(k).wait()

        @pl.when(k + AHEAD < STEPS)
        def _():
            fetch_g(k + AHEAD).start()

        for n in range(4):
            @pl.when(k == n)
            def _():
                fetch_a(n).start()

        signs = []
        for part in range(depth_g // LANE):
            start = k * depth_g + part * LANE
            first = (181 * sub + 7 * lane) + centred(181 * start + seeds_ref[1])
            second = (sub + 31 * lane) + start
            signs.append(signs_of(first, second))
        span = pl.ds(pl.multiple_of(k * depth_g, LANE), depth_g)
        g_acc[...] += jnp.dot(grad[:, span], jnp.concatenate(signs, axis=0), preferred_element_type=F32)
        return carry

    lax.fori_loop(0, STEPS, part_g, 0)
    for k in range(4):
        fetch_a(k).wait()
    a_acc[...] = lax.dot_general(
        s_a[...], act[...], (((1,), (1,)), ((), ())), preferred_element_type=F32
    )
    g = g_acc[...]
    a = a_acc[...]
    size = jnp.abs(g)
    g_up = exponent(jnp.max(size, axis=1, keepdims=True))
    g_across = exponent(jnp.max(size.T, axis=0, keepdims=True))
    a_up = exponent(jnp.max(jnp.abs(a), axis=0, keepdims=True))
    out_ref[0:ROWS_G, :] = jnp.round(g * jnp.exp2(14.0 - g_up)).astype(I32).astype(I16)
    a = jnp.round(a * jnp.exp2(14.0 - a_up)).astype(I32).astype(I16)
    total = g_across + a_up
    facts = [total.astype(I32)[:, LANE * k:LANE * (k + 1)] for k in range(4)]
    facts += [owner[:, LANE * k:LANE * (k + 1)] for k in range(4)]
    out_ref[ROWS_A:, :] = jnp.concatenate(facts + [jnp.zeros((8, LANE), I32)], axis=0).astype(I16)
    for k in range(4):
        out_ref[ROWS_G + KI * k:ROWS_G + KI * (k + 1), :] = a[:, LANE * k:LANE * (k + 1)]


def project(activations, out_grads, counts, seeds):
    depth_a = activations.shape[1]
    depth_g = out_grads.shape[1]
    return pl.pallas_call(
        project_kernel,
        out_shape=jax.ShapeDtypeStruct((ROWS, LANE), I16),
        in_specs=[
            pl.BlockSpec(memory_space=pltpu.SMEM),
            pl.BlockSpec(memory_space=pltpu.SMEM),
            pl.BlockSpec(memory_space=pl.ANY),
            pl.BlockSpec(memory_space=pl.ANY),
        ],
        out_specs=pl.BlockSpec(memory_space=pltpu.VMEM),
        scratch_shapes=[
            pltpu.VMEM((TOK, depth_a), BF16),
            pltpu.VMEM((TOK, depth_g), BF16),
            pltpu.VMEM((TOK, KO), F32),
            pltpu.VMEM((KI, TOK), F32),
            pltpu.VMEM((KI, depth_a), BF16),
            pltpu.SemaphoreType.DMA((4,)),
            pltpu.SemaphoreType.DMA((STEPS,)),
        ],
        compiler_params=pltpu.CompilerParams(vmem_limit_bytes=60 << 20),
        cost_estimate=pl.CostEstimate(flops=4 << 30, bytes_accessed=19 << 20, transcendentals=0),
        name="project",
    )(seeds, counts, activations, out_grads)


def form(held, slot, scale, target, row0, g_hi, g_lo, kin, a_work, hi_ref, lo_ref, lhs):
    g = held[slot, 0:ROWS_G, :].astype(I32).astype(F32)
    high = g.astype(BF16)
    g_hi[...] = high
    g_lo[...] = (g - high.astype(F32)).astype(BF16)
    facts = held[slot, ROWS_A:, :].astype(I32)
    for k in range(4):
        sizes = jnp.exp2(facts[k:k + 1, :].astype(F32)) * scale
        owner = facts[4 + k:5 + k, :]
        part = held[slot, ROWS_G + KI * k:ROWS_G + KI * (k + 1), :].astype(I32).astype(F32)
        a_work[k, 0:KI, :] = part * sizes
        a_work[k, KI:KI + 8, :] = jnp.broadcast_to(owner.astype(F32), (8, LANE))
        kin[k] = jnp.broadcast_to((owner >> 3).astype(F32), (LANE, LANE)).T.astype(BF16)
    sub = lax.broadcasted_iota(I32, (16, LANE), 0) & 7
    halves = []
    for group in range(8):
        low = 8 * group
        near = max(low, LANE * (group - 4)) // LANE
        far = (min(LANE * (group + 1), TOK - 8 * (7 - group)) - 1) // LANE
        a = a_work[near].reshape(KI // 8 + 1, 8, LANE)
        above, below = g_hi[LANE * near:LANE * (near + 1), :], g_lo[LANE * near:LANE * (near + 1), :]
        for k in range(near + 1, far + 1):
            owner = a_work[k, KI:KI + 8, :]
            mine = ((owner >= float(low)) & (owner < float(low + 8)))[None]
            a = jnp.where(mine, a_work[k].reshape(KI // 8 + 1, 8, LANE), a)
            mine = kin[k] == jnp.bfloat16(group)
            above = jnp.where(mine, g_hi[LANE * k:LANE * (k + 1), :], above)
            below = jnp.where(mine, g_lo[LANE * k:LANE * (k + 1), :], below)
        owner = jnp.concatenate([a[KI // 8]] * 2, axis=0)
        member = jnp.where(owner == (sub + low).astype(F32), 1.0, 0.0).astype(BF16)
        a = a[:KI // 8].reshape(KI, LANE)
        hi = a.astype(BF16).astype(F32)
        hi_ref[group] = hi
        lo_ref[group] = a - hi
        for j in range(0, KI, 2):
            for k, ref in enumerate((hi_ref, lo_ref)):
                rows = [jnp.broadcast_to(ref[group, j + n:j + n + 1, :], (8, LANE)) for n in range(2)]
                tile = jnp.concatenate(rows, axis=0).astype(BF16) * member
                lhs[group, 8 * j:8 * j + 16, LANE * k:LANE * (k + 1)] = tile
        weights = jnp.concatenate([above, below], axis=1)
        weights = jnp.concatenate([weights, weights], axis=0)
        both = jnp.dot(lhs[group], weights, preferred_element_type=F32)
        halves.append((both[:, :LANE] + both[:, LANE:]).reshape(KI, 8, LANE))
        if group % 2 == 1:
            features = jnp.concatenate(halves, axis=1).astype(BF16)
            halves = []
            at = pl.multiple_of(row0 + (group // 2) * 16, 16)
            for j in range(KI):
                target[pl.ds(at, 16), LANE * j:LANE * (j + 1)] = features[j]


def panel_kernel(n_row, n_col, packed_ref, out_ref, held, panel, g_hi, g_lo, kin, a_work, hi_ref, lo_ref, lhs,
                 send, arrive):
    p = lax.axis_index("row")
    core = lax.rem(lax.axis_index("col"), 2)
    q = lax.axis_index("col") // 2
    chips = n_col // 2

    def pair_q(m):
        return lax.rem(m + 4, 8)

    def ring_q(m, k):
        return (m // 4) * 4 + lax.rem(m + k, 4)

    def pair_p(m):
        return m + 1 - 2 * lax.rem(m, 2)

    def ring_p(m, k):
        return lax.rem(m + 2 * k, 8)

    sibling = (p, 2 * q + 1 - core)

    def place_of(panel, j):
        high = lax.rem(panel + j // 4 + panel // 4, 2)
        return 2 * lax.rem(panel // 2 + 2 + panel - j + 8, 4) + high

    def block_at(panel, m):
        x_lo = lax.rem(panel // 4 + panel + m, 2)
        return 4 * x_lo + lax.rem(panel + 2 + panel // 2 - m // 2 + 8, 4)

    start_place = (place_of(p, q), 2 * p + core)
    start_source = (q, 2 * block_at(q, p) + core)
    row_pair, row_up, row_down = [(p, 2 * m + core) for m in (pair_q(q), ring_q(q, 1), ring_q(q, 3))]
    col_pair, col_up, col_down = [(m, 2 * q + core) for m in (pair_p(p), ring_p(p, 1), ring_p(p, 3))]

    barrier = pltpu.get_barrier_semaphore()
    for other in (sibling, row_pair, row_up, row_down, col_pair, col_up, col_down):
        pl.semaphore_signal(barrier, inc=1, device_id=other, device_id_type=MESH)

    pl.semaphore_signal(barrier, inc=1, device_id=start_source, device_id_type=MESH)
    pl.semaphore_wait(barrier, 8)

    def row_slot(m):
        return 2 * m + core

    def col_slot(m):
        return n_col + 2 * m + core

    def copy(number, source, slot, device):
        return pltpu.make_async_remote_copy(
            src_ref=source, dst_ref=held.at[slot], send_sem=send.at[number], recv_sem=arrive.at[slot],
            device_id=device, device_id_type=MESH)

    def landed(slot):
        copy(0, held.at[slot], slot, sibling).wait_recv()

    own_slot = row_slot(q)
    rows = [q, pair_q(q), ring_q(q, 3), ring_q(q, 1), pair_q(ring_q(q, 3)), pair_q(ring_q(q, 1)), ring_q(q, 2),
            pair_q(ring_q(q, 2))]
    cols = [p, pair_p(p), ring_p(p, 3), ring_p(p, 1), pair_p(ring_p(p, 3)), pair_p(ring_p(p, 1)), ring_p(p, 2),
            pair_p(ring_p(p, 2))]
    row_next = {0: (row_pair, row_up, row_down), 1: (row_up, row_down), 2: (row_up,), 5: (row_down,)}
    col_next = {0: (col_pair, col_up, col_down), 1: (col_up, col_down), 2: (col_up,), 5: (col_down,)}

    def row_sends(i):
        slot = row_slot(rows[i])
        source = packed_ref if i == 0 else held.at[slot]
        base = 0 if i == 0 else sum(len(row_next.get(n, ())) + 1 for n in range(i))
        return [copy(base + n, source, slot, device) for n, device in enumerate(row_next.get(i, ()) + (sibling,))]

    def col_sends(i):
        slot = col_slot(cols[i])
        base = 16 + sum(len(col_next.get(n, ())) + 1 for n in range(i))
        moves = [copy(base + n, held.at[slot], slot, device) for n, device in enumerate(col_next.get(i, ()))]
        return moves, copy(base + len(moves), held.at[slot], slot, sibling), block_at(q, cols[i]) // 4 != core

    first_slot = col_slot(place_of(p, q))
    flip = copy(15, packed_ref, first_slot, start_place)
    flip.start()

    for move in row_sends(0):
        move.start()
    own = pltpu.make_async_copy(packed_ref, held.at[own_slot], arrive.at[own_slot])
    own.start()

    def row_step(i):
        landed(row_slot(rows[i]))
        if i > 0:
            for move in row_sends(i):
                move.start()

    def col_step(i):
        landed(col_slot(cols[i]))
        moves, across, wanted = col_sends(i)
        for move in moves:
            move.start()

        @pl.when(wanted)
        def _():
            across.start()

    plan = {0: [(row_step, 0)], 2: [(row_step, 1)], 3: [(col_step, 0)], 4: [(row_step, 2), (row_step, 3)],
            6: [(row_step, 4), (row_step, 5)], 8: [(col_step, 1)], 9: [(col_step, 2), (col_step, 3)],
            10: [(row_step, 6)], 12: [(row_step, 7)], 13: [(col_step, 5), (col_step, 4)], 15: [(col_step, 6)],
            20: [(col_step, 7)]}
    near = block_at(q, p) // 4 == core
    wanted_places = [jnp.where(near, cols[a], cols[b]) for a, b in ((0, 1), (2, 4), (3, 5), (6, 7))]
    unit = 2.0 ** -28 / 64.0
    scale = unit / math.sqrt(14336.0)

    def pick(values, i):
        value = values[0]
        for n in range(1, len(values)):
            value = jnp.where(i == n, values[n], value)
        return value

    def half(n):
        low = n_col * EX + 256 * n
        offsets = [pl.multiple_of(lax.rem(block_at(q, m), 4) * 128, 128) for m in wanted_places[2 * n:2 * n + 2]]

        def tile(t, carry):
            at = pl.multiple_of(t * 256, 256)
            total = None
            for k in range(4):
                term = lax.dot_general(
                    panel[pl.ds(at, 256), 2048 * k:2048 * (k + 1)], panel[low:low + 256, 2048 * k:2048 * (k + 1)],
                    (((1,), (1,)), ((), ())), preferred_element_type=F32)
                total = term if total is None else total + term
            for i in range(2):
                out_ref[pl.ds(at, 256), pl.ds(offsets[i], 128)] = total[:, 128 * i:128 * (i + 1)]
            return carry

        lax.fori_loop(0, 4, tile, 0)

    def block(k, carry):
        @pl.when(k == n_col + 4)
        def _():
            half(0)

        for at, steps in plan.items():
            @pl.when(k == at)
            def _():
                for step, i in steps:
                    step(i)

        is_row = k < n_col
        place = jnp.where(is_row, k, k - n_col) // 2
        other = lax.rem(k, 2)
        part = jnp.where(other == 0, core, 1 - core)
        m = jnp.where(is_row, pick(rows, place), pick(wanted_places, place))
        slot = jnp.where(is_row, 0, n_col) + 2 * m + part

        @pl.when(other == 1)
        def _():
            landed(slot)

        row0 = jnp.where(is_row, slot, n_col + 2 * place + part) * EX
        form(held, slot, jnp.where(is_row, scale / 64.0, scale / 128.0), panel, row0,
             g_hi, g_lo, kin, a_work, hi_ref, lo_ref, lhs)
        return carry

    lax.fori_loop(0, n_col + 8, block, 0)
    half(1)

    flip.wait_send()

    for i in range(chips):
        for move in row_sends(i):
            move.wait_send()
        moves, across, wanted = col_sends(i)
        for move in moves:
            move.wait_send()

        @pl.when(wanted)
        def _():
            across.wait_send()


def panels(packed, n_row, n_col):
    per = n_row
    rows, cols = n_col * EX, per * EX
    return pl.pallas_call(
        functools.partial(panel_kernel, n_row, n_col),
        out_shape=pltpu.VMEM((rows, cols), F32),
        in_specs=[pl.BlockSpec(memory_space=pl.ANY)],
        out_specs=pl.BlockSpec(memory_space=pltpu.VMEM),
        scratch_shapes=[
            pltpu.VMEM((2 * n_col, ROWS, LANE), I16),
            pltpu.VMEM((rows + cols, KO * KI), BF16),
            pltpu.VMEM((TOK, KO), BF16),
            pltpu.VMEM((TOK, KO), BF16),
            pltpu.VMEM((4, LANE, LANE), BF16),
            pltpu.VMEM((4, KI + 8, LANE), F32),
            pltpu.VMEM((8, KI, LANE), F32),
            pltpu.VMEM((8, KI, LANE), F32),
            pltpu.VMEM((8, 8 * KI, 2 * LANE), BF16),
            pltpu.SemaphoreType.DMA((32,)),
            pltpu.SemaphoreType.DMA((2 * n_col,)),
        ],
        compiler_params=pltpu.CompilerParams(
            collective_id=0, has_side_effects=True, vmem_limit_bytes=56 << 20),
        cost_estimate=pl.CostEstimate(flops=20 << 30, bytes_accessed=4 << 20, transcendentals=0),
        name="panels",
    )(packed)


def body(n_row, n_col, activations, out_grads, token_counts, proj_seeds):
    packed = project(activations, out_grads, token_counts, proj_seeds)
    return panels(packed, n_row, n_col)


def solution(mesh):
    return jax.shard_map(
        functools.partial(body, mesh.shape["row"], mesh.shape["col"]),
        mesh=mesh,
        in_specs=(P(("row", "col"), None), P(("row", "col"), None), P(("row", "col"), None), P()),
        out_specs=P("row", "col"),
        check_vma=False,
    )
```
